32 devices in a mesh: dp: 8 (over y, x, core), group: 4 (over z).
Axes of the slice: x: 2, y: 2, z: 4, core: 2. Of those that a mesh axis runs over, the one named last changes fastest.
Arguments:
- tokens: bfloat16 [8, 2048, 1088], P('dp', 'group'), may hold values from -6 to 6
- segments: int32 [8, 2048], P('dp'), may hold values from 0 to 10, as said below
- out_grad: bfloat16 [8, 2048, 1088], P('dp', 'group'), as said below
- norm1_gain: bfloat16 [1088], P('group'), may hold values from 0.5 to 1.5
- norm1_bias: bfloat16 [1088], P('group'), may hold values from -1.75 to 1.75
- w_query: bfloat16 [1088, 1088], P('group'), may hold values from -0.1875 to 0.1875
- query_bias: bfloat16 [1088], P('group'), may hold values from -3 to 3
- w_key: bfloat16 [1088, 1088], P('group'), may hold values from -0.1875 to 0.1875
- w_value: bfloat16 [1088, 1088], P('group'), may hold values from -0.1875 to 0.1875
- value_bias: bfloat16 [1088], P('group'), may hold values from -3 to 3
- w_out: bfloat16 [1088, 1088], P('group'), may hold values from -0.75 to 0.75
- out_bias: bfloat16 [1088], P('group'), may hold values from -3 to 3
- norm2_gain: bfloat16 [1088], P('group'), may hold values from 0.5 to 1.5
- norm2_bias: bfloat16 [1088], P('group'), may hold values from -1.75 to 1.75
- w_fc: bfloat16 [1088, 4352], P('group'), may hold values from -0.1875 to 0.1875
- fc_bias: bfloat16 [4352], P('group'), may hold values from -3 to 3
- w_proj: bfloat16 [4352, 1088], P('group'), may hold values from -0.09375 to 0.09375
- proj_bias: bfloat16 [1088], P('group'), may hold values from -3 to 3
Outputs:
- activations: float32 [8, 2048, 1088], P('dp', 'group')
- tokens_grad: float32 [8, 2048, 1088], P('dp', 'group')
- norm1_gain_grad: float32 [1088], P('group')
- norm1_bias_grad: float32 [1088], P('group')
- w_query_grad: float32 [1088, 1088], P('group')
- query_bias_grad: float32 [1088], P('group')
- w_key_grad: float32 [1088, 1088], P('group')
- w_value_grad: float32 [1088, 1088], P('group')
- value_bias_grad: float32 [1088], P('group')
- w_out_grad: float32 [1088, 1088], P('group')
- out_bias_grad: float32 [1088], P('group')
- norm2_gain_grad: float32 [1088], P('group')
- norm2_bias_grad: float32 [1088], P('group')
- w_fc_grad: float32 [1088, 4352], P('group')
- fc_bias_grad: float32 [4352], P('group')
- w_proj_grad: float32 [4352, 1088], P('group')
- proj_bias_grad: float32 [1088], P('group')
The draws below stay inside these ranges and needn't reach their ends.
Inputs may be any that keep to these rules, and one draw needn't show every extreme that they name: `segments`: segment numbers start at 0 in each sequence and rise by one at each document's start; every segment but the last holds 200 to 2000 tokens, the last is padding of 1 to 2000 tokens. `out_grad`: zero on every token of a sequence's last segment.
All inputs are finite; a program needn't handle non-finite values.
Results may differ from the reference program's by a relative error of at most 0.02.
Values may be sent and summed in bfloat16 or wider, within the bound.
No kernel may reach another device: no remote copies, remote signals or barrier semaphores. Data moves between devices by JAX's collectives and lax.ppermute only.
A program may use at most 256 MiB of HBM per device.

```python
import jax
import jax.numpy as jnp
from jax import lax

D = 1088
FF = 4352
HEADS = 17
HEAD = 64
SEQ_LEN = 2048
KB = 512
BATCH = 8
DOC_MIN = 200
DOC_MAX = 2000


def segment_ids(key):
    doc_lengths = jax.random.randint(key, (BATCH, 12), DOC_MIN, DOC_MAX + 1)
    row_index = jnp.arange(BATCH, dtype=jnp.int32)[:, None]
    doc_lengths = jnp.where(row_index == 0, DOC_MIN, doc_lengths)
    doc_ends = jnp.cumsum(doc_lengths, axis=1)
    positions = jnp.arange(SEQ_LEN, dtype=jnp.int32)
    return jnp.sum((doc_ends[:, None, :] <= positions[None, :, None]).astype(jnp.int32), axis=2)


def draw_segments(key, part):
    return segment_ids(jax.random.fold_in(key, 1))


def draw_out_grad(key, part):
    seg_ids = segment_ids(jax.random.fold_in(key, 1))
    live = seg_ids != seg_ids[:, -1:]
    noise = jax.random.normal(jax.random.fold_in(key, 2), (BATCH, SEQ_LEN, D), jnp.float32)
    return jnp.where(live[:, :, None], noise, 0.0).astype(jnp.bfloat16)


def shard_levels(key, dims, split, least, top_value):
    def one(position, parts):
        heights = jax.random.uniform(jax.random.fold_in(jax.random.fold_in(key, 6), position), (parts,), jnp.float32, least / len(split), top_value / len(split))
        return jnp.repeat(jnp.exp(heights), dims[position] // parts).reshape((-1,) + (1,) * (len(dims) - position - 1))

    level = one(*split[0])
    for cut in split[1:]:
        level = level * one(*cut)
    return level


def normal_values(rng, shape, width, reach, pieces=(), kind=jnp.bfloat16):
    array = width * jax.random.normal(rng, shape, jnp.float32)
    if pieces:
        array = array * shard_levels(rng, shape, pieces, -0.22, 0.18)
    return jnp.clip(array, -reach, reach).astype(kind)


def setup_inputs(seed: int = 0) -> dict:
    key_of = jax.random.split(jax.random.key(seed), 19)
    return {
        "tokens": normal_values(key_of[0], (BATCH, SEQ_LEN, D), 1.0, 6.0, ((0, 8), (1, 4))),
        "segments": draw_segments(jax.random.fold_in(key_of[18], 71), 0),
        "out_grad": draw_out_grad(jax.random.fold_in(key_of[18], 71), 0),
        "norm1_gain": jnp.clip(1.0 + 0.1 * jax.random.normal(key_of[3], (D,), jnp.float32), 0.5, 1.5).astype(jnp.bfloat16),
        "norm1_bias": normal_values(key_of[4], (D,), 0.3, 1.75, ((0, 4),)),
        "w_query": normal_values(key_of[5], (D, D), D ** -0.5, 0.1875, ((0, 4),)),
        "query_bias": normal_values(key_of[6], (D,), 0.5, 3.0, ((0, 4),)),
        "w_key": normal_values(key_of[7], (D, D), D ** -0.5, 0.1875, ((0, 4),)),
        "w_value": normal_values(key_of[8], (D, D), D ** -0.5, 0.1875, ((0, 4),)),
        "value_bias": normal_values(key_of[9], (D,), 0.5, 3.0, ((0, 4),)),
        "w_out": normal_values(key_of[10], (D, D), (D // 16) ** -0.5, 0.75, ((0, 4),)),
        "out_bias": normal_values(key_of[11], (D,), 0.5, 3.0, ((0, 4),)),
        "norm2_gain": jnp.clip(1.0 + 0.1 * jax.random.normal(key_of[12], (D,), jnp.float32), 0.5, 1.5).astype(jnp.bfloat16),
        "norm2_bias": normal_values(key_of[13], (D,), 0.3, 1.75, ((0, 4),)),
        "w_fc": normal_values(key_of[14], (D, FF), D ** -0.5, 0.1875, ((0, 4),)),
        "fc_bias": normal_values(key_of[15], (FF,), 0.5, 3.0, ((0, 4),)),
        "w_proj": normal_values(key_of[16], (FF, D), FF ** -0.5, 0.09375, ((0, 4),)),
        "proj_bias": normal_values(key_of[17], (D,), 0.5, 3.0, ((0, 4),)),
    }


EPSILON = 1e-05
NEG_FILL = -1e+30
HIGH = lax.Precision.HIGHEST

@jax.custom_vjp
def low(v):
    return lax.optimization_barrier(v.astype(jnp.bfloat16)).astype(jnp.float32)

@jax.custom_vjp
def low_back(v):
    return v

def low_keep(v):
    return (low(v), None)

def low_pass(kept, grad):
    return (grad,)

def back_keep(v):
    return (v, None)

def back_low(kept, grad):
    return (low(grad),)
low.defvjp(low_keep, low_pass)
low_back.defvjp(back_keep, back_low)

def layer_norm(values, gain, shift):
    center = values - lax.optimization_barrier(jnp.mean(values, axis=-1, keepdims=True))
    spread = lax.optimization_barrier(jnp.mean(center * center, axis=-1, keepdims=True))
    return center * lax.rsqrt(spread + EPSILON) * gain + shift

def matmul(left, right):
    return jnp.dot(left, right, precision=HIGH, preferred_element_type=jnp.float32)

def attend_block(query_block, query_pos, query_seg, keys_heads, values_heads, seg_seq):
    scores = low_back(jnp.einsum('hqe,hke->hqk', query_block, keys_heads, precision=HIGH) * HEAD ** (-0.5))
    key_pos = jnp.arange(SEQ_LEN, dtype=jnp.int32)
    keep_mask = (key_pos[None, :] <= query_pos[:, None]) & (seg_seq[None, :] == query_seg[:, None])
    scores = jnp.where(keep_mask[None], scores, NEG_FILL)
    peak = lax.optimization_barrier(jnp.max(scores, axis=-1, keepdims=True))
    weights = jnp.exp(scores - peak)
    probs = weights / lax.optimization_barrier(jnp.sum(weights, axis=-1, keepdims=True))
    return jnp.einsum('hqk,hke->hqe', low(probs), values_heads, precision=HIGH)

def split_heads(values):
    return values.reshape(SEQ_LEN, HEADS, HEAD).transpose(1, 0, 2)

def forward(seq_in, seg_seq, param_set):
    norm1_gain, norm1_bias, w_query, query_bias, w_key, w_value, value_bias, w_out, out_bias, norm2_gain, norm2_bias, w_fc, fc_bias, w_proj, proj_bias = param_set
    normed_one = low(layer_norm(seq_in, norm1_gain, norm1_bias))
    queries = low_back(low(matmul(normed_one, w_query) + query_bias))
    keys = low_back(low(matmul(normed_one, w_key)))
    values = low_back(low(matmul(normed_one, w_value) + value_bias))
    keys_heads = split_heads(keys)
    values_heads = split_heads(values)
    block_count = SEQ_LEN // KB
    query_blocks = split_heads(queries).reshape(HEADS, block_count, KB, HEAD).transpose(1, 0, 2, 3)
    pos_blocks = jnp.arange(SEQ_LEN, dtype=jnp.int32).reshape(block_count, KB)
    seg_blocks = seg_seq.reshape(block_count, KB)

    def one_block(items):
        return attend_block(items[0], items[1], items[2], keys_heads, values_heads, seg_seq)
    attended = lax.map(jax.checkpoint(one_block), (query_blocks, pos_blocks, seg_blocks))
    attended = attended.transpose(0, 2, 1, 3).reshape(SEQ_LEN, D)
    attended = low_back(low(attended))
    resid = seq_in + low_back(matmul(attended, w_out) + out_bias)
    normed_two = low(layer_norm(resid, norm2_gain, norm2_bias))
    pre_act = low_back(matmul(normed_two, w_fc) + fc_bias)
    hidden = low(jax.nn.gelu(pre_act, approximate=True))
    return resid + low_back(matmul(hidden, w_proj) + proj_bias)

def reference(tokens, segments, out_grad, norm1_gain, norm1_bias, w_query, query_bias, w_key, w_value, value_bias, w_out, out_bias, norm2_gain, norm2_bias, w_fc, fc_bias, w_proj, proj_bias):
    param_set = tuple((param.astype(jnp.float32) for param in (norm1_gain, norm1_bias, w_query, query_bias, w_key, w_value, value_bias, w_out, out_bias, norm2_gain, norm2_bias, w_fc, fc_bias, w_proj, proj_bias)))

    def per_sequence(grad_sums, items):
        seq_in, seg_seq, seq_cot = items

        def layer_at(seq_float, params_now):
            return forward(seq_float, seg_seq, params_now)
        acts, pullback = jax.vjp(layer_at, seq_in.astype(jnp.float32), param_set)
        in_grad, param_grads = pullback(seq_cot.astype(jnp.float32))
        return (jax.tree.map(jnp.add, grad_sums, param_grads), (acts, in_grad))
    zero_sums = tuple((jnp.zeros_like(param) for param in param_set))
    totals, outs_pair = lax.scan(per_sequence, zero_sums, (tokens, segments, out_grad))
    return (outs_pair[0], outs_pair[1], totals[0], totals[1], totals[2], totals[3], totals[4], totals[5], totals[6], totals[7], totals[8], totals[9], totals[10], totals[11], totals[12], totals[13], totals[14])
```

```python
from functools import partial

import jax
import jax.numpy as jnp
from jax import lax
from jax.experimental import pallas as pl
from jax.experimental.pallas import tpu as pltpu
from jax.sharding import PartitionSpec as P

HEAD = 64
LANES = 128
EPSILON = 1e-05
NEG_FILL = -1e30
F32 = jnp.float32
BF16 = jnp.bfloat16
SCALE = HEAD ** (-0.5)


def lane_mask(shape, head):
    lane = lax.broadcasted_iota(jnp.int32, shape, 1)
    return (lane < HEAD) if head == 0 else (lane >= HEAD)


def keep_of(tile_base, tile_len, low_row, own_base):
    span_len = low_row.shape[1]
    key_pos = tile_base + lax.broadcasted_iota(jnp.int32, (tile_len, span_len), 0)
    query_pos = own_base + lax.broadcasted_iota(jnp.int32, (tile_len, span_len), 1)
    return (key_pos >= low_row) & (key_pos <= query_pos)


def tile_loops(bounds_ref, tile, own_tile, tile_count):
    low_tile = bounds_ref[0]
    mid_tile = bounds_ref[1]
    lax.fori_loop(low_tile, mid_tile, lambda t, c: tile(t, True), None)
    lax.fori_loop(mid_tile, own_tile, lambda t, c: tile(t, False), None)
    for t in range(own_tile, tile_count):
        tile(t, True)


def forward_kernel(
    tile_len, last_half, bounds_ref, q_ref, k_ref, v_ref, low_ref, o_ref, lse_ref, max_ref, sum_ref, acc_ref
):
    span_len = q_ref.shape[0]
    key_len = k_ref.shape[0]
    own_base = key_len - span_len
    pair = pl.program_id(0)
    last = pair == pl.num_programs(0) - 1
    valid = jnp.where(last, last_half, LANES)
    q_t = (q_ref[...].astype(F32) * SCALE).T
    row = lax.broadcasted_iota(jnp.int32, q_t.shape, 0)
    heads = (
        jnp.where(row < HEAD, q_t, 0.0).astype(BF16),
        jnp.where((row >= HEAD) & (row < valid), q_t, 0.0).astype(BF16),
    )
    max_ref[...] = jnp.full_like(max_ref, NEG_FILL)
    sum_ref[...] = jnp.zeros_like(sum_ref)
    acc_ref[...] = jnp.zeros_like(acc_ref)

    def tile(t, masked):
        base = t * tile_len
        rows = pl.ds(pl.multiple_of(base, tile_len), tile_len)
        lane = lax.broadcasted_iota(jnp.int32, (tile_len, LANES), 1)
        k_tile = jnp.where(lane < valid, k_ref[rows, :], jnp.zeros((), BF16))
        v_t = v_ref[rows, :].T
        if masked:
            keep = keep_of(base, tile_len, low_ref[...], own_base)

        def one(head):
            scores = jnp.dot(k_tile, heads[head], preferred_element_type=F32)
            if masked:
                scores = jnp.where(keep, scores, NEG_FILL)
            old_max = max_ref[head]
            new_max = jnp.maximum(old_max, jnp.max(scores, axis=0, keepdims=True))
            shrink = jnp.exp(old_max - new_max)
            probs = jnp.exp(scores - new_max)
            max_ref[head] = new_max
            sum_ref[head] = sum_ref[head] * shrink + jnp.sum(probs, axis=0, keepdims=True)
            acc_ref[head] = acc_ref[head] * shrink + jnp.dot(
                v_t[head * HEAD : (head + 1) * HEAD], probs.astype(BF16), preferred_element_type=F32
            )

        one(0)
        pl.when(valid > HEAD)(lambda: one(1))

    tile_loops(bounds_ref, tile, own_base // tile_len, key_len // tile_len)
    safe = jnp.where(sum_ref[...] > 0, sum_ref[...], 1.0)
    out = jnp.concatenate([acc_ref[0] / safe[0], acc_ref[1] / safe[1]], axis=0)
    o_ref[...] = out.T.astype(BF16)
    lse_ref[0] = jnp.concatenate([max_ref[0] + jnp.log(safe[0]), max_ref[1] + jnp.log(safe[1])], axis=0)


def backward_kernel(
    tile_len, last_half, bounds_ref, q_ref, k_ref, v_ref, g_ref, o_ref, lse_ref, low_ref, dq_ref, dk_ref, dv_ref, acc_ref
):
    span_len = q_ref.shape[0]
    key_len = k_ref.shape[0]
    own_base = key_len - span_len
    pair = pl.program_id(0)
    last = pair == pl.num_programs(0) - 1
    valid = jnp.where(last, last_half, LANES)
    lane = lax.broadcasted_iota(jnp.int32, (span_len, LANES), 1)
    q_now = jnp.where(lane < valid, q_ref[...].astype(F32) * SCALE, 0.0)
    g_now = jnp.where(lane < valid, g_ref[...].astype(F32), 0.0)
    o_now = jnp.where(lane < valid, o_ref[...].astype(F32), 0.0)
    q_t, g_t, o_t = q_now.T, g_now.T, o_now.T
    row = lax.broadcasted_iota(jnp.int32, q_t.shape, 0)
    prod = g_t * o_t
    part = []
    for head in range(2):
        row_ok = (row < HEAD) if head == 0 else (row >= HEAD)
        lane_ok = (lane < HEAD) if head == 0 else (lane >= HEAD)
        part.append(
            (
                jnp.where(row_ok, q_t, 0.0).astype(BF16),
                jnp.where(row_ok, g_t, 0.0).astype(BF16),
                jnp.where(lane_ok, q_now, 0.0).astype(BF16),
                jnp.where(lane_ok, g_now, 0.0).astype(BF16),
                jnp.sum(prod[head * HEAD : (head + 1) * HEAD], axis=0, keepdims=True),
                lse_ref[0, head : head + 1],
            )
        )
    acc_ref[...] = jnp.zeros_like(acc_ref)

    def clear(t, carry):
        rows = pl.ds(pl.multiple_of(t * tile_len, tile_len), tile_len)
        dk_ref[rows, :] = jnp.zeros((tile_len, LANES), BF16)
        dv_ref[rows, :] = jnp.zeros((tile_len, LANES), BF16)
        return carry

    lax.fori_loop(0, bounds_ref[0], clear, None)

    def tile(t, masked):
        base = t * tile_len
        rows = pl.ds(pl.multiple_of(base, tile_len), tile_len)
        lane_k = lax.broadcasted_iota(jnp.int32, (tile_len, LANES), 1)
        k_tile = jnp.where(lane_k < valid, k_ref[rows, :], jnp.zeros((), BF16))
        v_tile = jnp.where(lane_k < valid, v_ref[rows, :], jnp.zeros((), BF16))
        k_t = k_tile.T
        if masked:
            keep = keep_of(base, tile_len, low_ref[...], own_base)

        def one(head):
            qh_t, gh_t, qh, gh, delta, lse = part[head]
            scores = jnp.dot(k_tile, qh_t, preferred_element_type=F32)
            probs = jnp.exp(scores - lse)
            if masked:
                probs = jnp.where(keep, probs, 0.0)
            dprobs = jnp.dot(v_tile, gh_t, preferred_element_type=F32)
            dscores = (probs * (dprobs - delta)).astype(BF16)
            dv = jnp.dot(probs.astype(BF16), gh, preferred_element_type=F32)
            dk = jnp.dot(dscores, qh, preferred_element_type=F32)
            acc_ref[head] += jnp.dot(
                k_t[head * HEAD : (head + 1) * HEAD], dscores, preferred_element_type=F32
            )
            return dk, dv

        def write(dk, dv):
            dk_ref[rows, :] = dk.astype(BF16)
            dv_ref[rows, :] = dv.astype(BF16)

        @pl.when(valid > HEAD)
        def _():
            dk_a, dv_a = one(0)
            dk_b, dv_b = one(1)
            write(dk_a + dk_b, dv_a + dv_b)

        @pl.when(valid <= HEAD)
        def _():
            write(*one(0))

    tile_loops(bounds_ref, tile, own_base // tile_len, key_len // tile_len)
    dq_ref[...] = (jnp.concatenate([acc_ref[0], acc_ref[1]], axis=0).T * SCALE).astype(BF16)


def attend_specs(span_len, key_len, width):
    pairs = pl.cdiv(width, LANES)
    tile_len = 256 if span_len % 256 == 0 else span_len
    last_half = width - (pairs - 1) * LANES
    own = pl.BlockSpec((span_len, LANES), lambda p, b: (0, p))
    keys = pl.BlockSpec((key_len, LANES), lambda p, b: (0, p))
    low = pl.BlockSpec((1, span_len), lambda p, b: (0, 0))
    lse = pl.BlockSpec((1, 2, span_len), lambda p, b: (p, 0, 0))
    return pairs, tile_len, last_half, own, keys, low, lse


def attend_forward(queries, keys, values, low_row, bounds):
    span_len, width = queries.shape
    key_len = keys.shape[0]
    pairs, tile_len, last_half, own, key_spec, low_spec, lse_spec = attend_specs(span_len, key_len, width)
    return pl.pallas_call(
        partial(forward_kernel, tile_len, last_half),
        out_shape=(
            jax.ShapeDtypeStruct((span_len, width), BF16),
            jax.ShapeDtypeStruct((pairs, 2, span_len), F32),
        ),
        grid_spec=pltpu.PrefetchScalarGridSpec(
            num_scalar_prefetch=1,
            grid=(pairs,),
            in_specs=[own, key_spec, key_spec, low_spec],
            out_specs=(own, lse_spec),
            scratch_shapes=[
                pltpu.VMEM((2, 1, span_len), F32),
                pltpu.VMEM((2, 1, span_len), F32),
                pltpu.VMEM((2, HEAD, span_len), F32),
            ],
        ),
        cost_estimate=pl.CostEstimate(
            flops=4 * span_len * key_len * width, bytes_accessed=4 * key_len * width, transcendentals=span_len * key_len * 17
        ),
        compiler_params=pltpu.CompilerParams(vmem_limit_bytes=40 * 1024 * 1024),
        name="attend_forward",
    )(bounds, queries, keys, values, low_row)


def attend_backward(queries, keys, values, out_grad, attended, lse, low_row, bounds):
    span_len, width = queries.shape
    key_len = keys.shape[0]
    pairs, tile_len, last_half, own, key_spec, low_spec, lse_spec = attend_specs(span_len, key_len, width)
    return pl.pallas_call(
        partial(backward_kernel, tile_len, last_half),
        out_shape=(
            jax.ShapeDtypeStruct((span_len, width), BF16),
            jax.ShapeDtypeStruct((key_len, width), BF16),
            jax.ShapeDtypeStruct((key_len, width), BF16),
        ),
        grid_spec=pltpu.PrefetchScalarGridSpec(
            num_scalar_prefetch=1,
            grid=(pairs,),
            in_specs=[own, key_spec, key_spec, own, own, lse_spec, low_spec],
            out_specs=(own, key_spec, key_spec),
            scratch_shapes=[pltpu.VMEM((2, HEAD, span_len), F32)],
        ),
        cost_estimate=pl.CostEstimate(
            flops=10 * span_len * key_len * width, bytes_accessed=8 * key_len * width, transcendentals=span_len * key_len * 17
        ),
        compiler_params=pltpu.CompilerParams(vmem_limit_bytes=40 * 1024 * 1024),
        name="attend_backward",
    )(bounds, queries, keys, values, out_grad, attended, lse, low_row)


def along_group(x, step, count, wrap):
    pairs = [(i, (i + step) % count) for i in range(count) if wrap or 0 <= i + step < count]
    return lax.ppermute(x, "group", pairs)


def flip(x, bit, count):
    return lax.ppermute(x, "dp", [(i, i ^ bit) for i in range(count)])


CORE, ACROSS, DOWN = 1, 2, 4


def pick(x, index, axis=0):
    return lax.dynamic_index_in_dim(x, index, axis, keepdims=False)


def put(x, part, index):
    start = tuple(index) + (0,) * (x.ndim - len(index))
    part = part.reshape((1,) * len(index) + part.shape)
    return lax.dynamic_update_slice(x, part, start)


def plane_share(mine, count):
    cut = (mine.shape[1] // 2 + 7) // 8 * 8
    from_x = flip(mine, ACROSS, count)
    from_y = flip(mine, DOWN, count)
    diag_low = flip(from_x[:, :cut], DOWN, count)
    diag_high = flip(from_y[:, cut:], ACROSS, count)
    return mine, from_x, from_y, jnp.concatenate([diag_low, diag_high], axis=1)


def fast_gather(own, place, count, groups, here):
    chip, core, z = here
    piece = pick(pick(own, chip), core)
    ring = []
    hop = piece
    for _ in range(groups - 1):
        hop = along_group(hop, 1, groups, True)
        ring.append(hop)
    shares = plane_share(jnp.stack(ring), count)
    mine = jnp.stack(shares)
    other = flip(mine, CORE, count)
    rows, cols = piece.shape
    whole = jnp.zeros((4, groups, 2, rows, cols), piece.dtype)
    whole = lax.dynamic_update_slice(whole, own[:, None], (0, z, 0, 0, 0))
    for k in range(4):
        for step in range(groups - 1):
            plane = lax.rem(z - step - 1 + groups, groups)
            whole = put(whole, mine[k, step], (chip ^ k, plane, core))
            whole = put(whole, other[k, step], (chip ^ k, plane, 1 - core))
    return whole


def fast_reduce(parts, count, groups, here):
    chip, core, z = here
    got = flip(pick(parts, 1 - core, 2), CORE, count)
    half = (pick(parts, core, 2).astype(F32) + got.astype(F32)).astype(BF16)
    cut = groups // 2
    to_own, to_x, to_y, to_diag = (pick(half, chip ^ k) for k in range(4))
    via_x = flip(to_diag[:cut], ACROSS, count)
    via_y = flip(to_diag[cut:], DOWN, count)
    send_y = jnp.concatenate([to_y[:cut] + via_x, to_y[cut:]])
    send_x = jnp.concatenate([to_x[:cut], to_x[cut:] + via_y])
    from_x = flip(send_x, ACROSS, count)
    from_y = flip(send_y, DOWN, count)
    mine = to_own.astype(F32) + from_x.astype(F32) + from_y.astype(F32)
    hop = None
    for step in range(1, groups):
        term = pick(mine, lax.rem(z - step + groups, groups))
        if hop is not None:
            term = term + hop.astype(F32)
        hop = along_group(term.astype(BF16), 1, groups, True)
    total = (pick(mine, z) + hop.astype(F32)).astype(BF16)
    shares = jnp.concatenate(plane_share(total[None], count))
    other = flip(shares, CORE, count)
    out = jnp.zeros((4, 2) + total.shape, BF16)
    for k in range(4):
        out = put(out, shares[k], (chip ^ k, core))
        out = put(out, other[k], (chip ^ k, 1 - core))
    return out


def mean_spread(values):
    center = values - jnp.mean(values, axis=-1, keepdims=True)
    spread = jnp.mean(center * center, axis=-1, keepdims=True)
    return center, lax.rsqrt(spread + EPSILON)


def layer_norm(values, gain, shift):
    center, scale = mean_spread(values)
    return center * scale * gain + shift


def layer_norm_back(values, gain, grad):
    center, scale = mean_spread(values)
    unit = center * scale
    inner = grad * gain
    back = scale * (
        inner
        - jnp.mean(inner, axis=-1, keepdims=True)
        - unit * jnp.mean(inner * unit, axis=-1, keepdims=True)
    )
    return back, jnp.sum(grad * unit, axis=0), jnp.sum(grad, axis=0)


def row_sum(values):
    return jnp.sum(values.astype(F32), axis=0)


def matmul(left, right):
    return jnp.dot(left, right, preferred_element_type=F32)


def weight_grad(left, right):
    return jnp.einsum("ra,rb->ab", left, right, preferred_element_type=F32).astype(BF16)


def back_through(grad_rows, weight):
    return jnp.einsum("rb,ab->ra", grad_rows, weight, preferred_element_type=F32)


def on_device(
    count,
    groups,
    tokens,
    segments,
    out_grad,
    norm1_gain,
    norm1_bias,
    w_query,
    query_bias,
    w_key,
    w_value,
    value_bias,
    w_out,
    out_bias,
    norm2_gain,
    norm2_bias,
    w_fc,
    fc_bias,
    w_proj,
    proj_bias,
):
    _, span_len, width = tokens.shape
    shard = width // groups
    chunks = w_fc.shape[1] // width
    key_len = segments.shape[1]
    z = lax.axis_index("group")
    place = lax.axis_index("dp")
    fast = count == 8 and groups == 4 and chunks == 4
    here = (place // 2, lax.rem(place, 2), z)

    small = jnp.concatenate(
        [norm1_gain, norm1_bias, query_bias, value_bias, out_bias, norm2_gain, norm2_bias, proj_bias, fc_bias]
    )
    small_all = lax.all_gather(small, "group")
    vectors = small_all[:, : 8 * shard].reshape(groups, 8, shard).transpose(1, 0, 2).reshape(8, width)
    gain_one, shift_one, bias_q, bias_v, bias_o, gain_two, shift_two, bias_p = vectors.astype(F32)
    bias_fc = small_all[:, 8 * shard :].astype(F32).reshape(chunks, 1, width)

    if fast:
        half = shard // 2
        attn_own = jnp.stack([w_query, w_key, w_value, w_out]).reshape(4, 2, half, width)
        fc_own = w_fc.reshape(2, half, chunks, width).transpose(2, 0, 1, 3)
        proj_own = w_proj.reshape(4, 2, half, width)
        attn = fast_gather(attn_own, place, count, groups, here).reshape(4, width, width)
        full_fc = fast_gather(fc_own, place, count, groups, here).reshape(4, width, width)
        full_proj = fast_gather(proj_own, place, count, groups, here).transpose(1, 0, 2, 3, 4).reshape(4, width, width)
        full_q, full_k, full_v, full_o = attn[0], attn[1], attn[2], attn[3]
    else:
        gather = partial(lax.all_gather, axis_name="group", axis=0, tiled=True)
        full_q, full_k, full_v, full_o = (gather(w) for w in (w_query, w_key, w_value, w_out))
        full_fc = gather(w_fc).reshape(width, chunks, width).transpose(1, 0, 2)
        full_proj = gather(w_proj).reshape(chunks, width, width)

    mine = tokens[0]
    hops = [mine]
    for _ in range(groups - 1):
        hops.append(along_group(hops[-1], 1, groups, False))
    reach = jnp.concatenate(hops[::-1]).astype(F32)
    own_base = key_len - span_len
    inputs = mine.astype(F32)

    seg = segments[0]
    seg_mine = lax.dynamic_slice_in_dim(seg, z * span_len, span_len)
    low_row = jnp.sum((seg[None, :] < seg_mine[:, None]).astype(jnp.int32), axis=1)
    low_row = low_row + (groups - 1 - z) * span_len
    tile_len = 256 if span_len % 256 == 0 else span_len
    low_tile = low_row[0] // tile_len
    mid_tile = jnp.clip((low_row[-1] + tile_len - 1) // tile_len, low_tile, own_base // tile_len)
    bounds = jnp.stack([low_tile, mid_tile]).astype(jnp.int32)
    low_row = low_row[None]

    normed_all = layer_norm(reach, gain_one, shift_one).astype(BF16)
    normed_one = layer_norm(inputs, gain_one, shift_one).astype(BF16)
    queries = (matmul(normed_one, full_q) + bias_q).astype(BF16)
    keys = matmul(normed_all, full_k).astype(BF16)
    values = (matmul(normed_all, full_v) + bias_v).astype(BF16)
    attended, lse = attend_forward(queries, keys, values, low_row, bounds)
    resid = inputs + matmul(attended, full_o) + bias_o
    normed_two = layer_norm(resid, gain_two, shift_two).astype(BF16)
    pre_act = jnp.einsum("td,jdf->jtf", normed_two, full_fc, preferred_element_type=F32) + bias_fc
    gelu_tanh = partial(jax.nn.gelu, approximate=True)
    hidden, gelu_back = jax.vjp(gelu_tanh, pre_act)
    hidden = hidden.astype(BF16)
    activations = resid + jnp.einsum("jtf,jfd->td", hidden, full_proj, preferred_element_type=F32) + bias_p

    cot = out_grad[0]
    proj_bias_grad = row_sum(cot)
    proj_grad = jnp.einsum("jtf,td->jfd", hidden, cot, preferred_element_type=F32).astype(BF16)
    hidden_grad = jnp.einsum("td,jfd->jtf", cot, full_proj, preferred_element_type=F32)
    pre_grad = gelu_back(hidden_grad)[0].astype(BF16)
    fc_bias_grad = jnp.sum(pre_grad.astype(F32), axis=1)
    fc_grad = jnp.einsum("td,jtf->jdf", normed_two, pre_grad, preferred_element_type=F32).astype(BF16)
    normed_two_grad = jnp.einsum("jtf,jdf->td", pre_grad, full_fc, preferred_element_type=F32)
    resid_part, gain_two_grad, shift_two_grad = layer_norm_back(resid, gain_two, normed_two_grad)
    resid_grad = cot.astype(F32) + resid_part
    resid_low = resid_grad.astype(BF16)
    out_bias_grad = row_sum(resid_low)
    out_w_grad = weight_grad(attended, resid_low)
    attended_grad = back_through(resid_low, full_o).astype(BF16)
    dqueries, dkeys, dvalues = attend_backward(queries, keys, values, attended_grad, attended, lse, low_row, bounds)
    query_bias_grad = row_sum(dqueries)
    value_bias_grad = row_sum(dvalues)
    q_grad = weight_grad(normed_one, dqueries)
    k_grad = weight_grad(normed_all, dkeys)
    v_grad = weight_grad(normed_all, dvalues)
    norm_terms = back_through(dkeys, full_k) + back_through(dvalues, full_v)
    moving = None
    for step in range(groups - 1):
        term = norm_terms[step * span_len : (step + 1) * span_len]
        if moving is not None:
            term = term + moving.astype(F32)
        moving = along_group(term.astype(BF16), -1, groups, False)
    normed_one_grad = back_through(dqueries, full_q) + norm_terms[own_base:] + moving.astype(F32)
    input_part, gain_one_grad, shift_one_grad = layer_norm_back(inputs, gain_one, normed_one_grad)
    tokens_grad = resid_grad + input_part

    vector_grads = jnp.stack(
        [
            gain_one_grad,
            shift_one_grad,
            query_bias_grad,
            value_bias_grad,
            out_bias_grad,
            gain_two_grad,
            shift_two_grad,
            proj_bias_grad,
        ]
    )
    vector_grads = vector_grads.reshape(8, groups, shard).transpose(1, 0, 2).reshape(groups, 8 * shard)
    vector_grads = jnp.concatenate([vector_grads, fc_bias_grad.reshape(groups, -1)], axis=1)
    vector_sums = pick(lax.psum(vector_grads, ("dp", "group")), z)
    eight = vector_sums[: 8 * shard].reshape(8, shard)
    fc_bias_sum = vector_sums[8 * shard :]
    if fast:
        proj_parts = proj_grad.reshape(groups, 4, 2, half, width).transpose(1, 0, 2, 3, 4)
        proj_sum = fast_reduce(proj_parts, count, groups, here).reshape(4 * shard, width).astype(F32)
        fc_sum = fast_reduce(fc_grad.reshape(4, groups, 2, half, width), count, groups, here)
        fc_sum = fc_sum.reshape(4, shard, width).transpose(1, 0, 2).reshape(shard, 4 * width).astype(F32)
        attn_parts = jnp.stack([q_grad, k_grad, v_grad, out_w_grad]).reshape(4, groups, 2, half, width)
        attn_sum = fast_reduce(attn_parts, count, groups, here).reshape(4, shard, width).astype(F32)
        q_sum, k_sum, v_sum, out_sum = attn_sum[0], attn_sum[1], attn_sum[2], attn_sum[3]
    else:

        def whole_sum(part):
            part = lax.psum_scatter(part, "group", scatter_dimension=0, tiled=True)
            return lax.psum(part.astype(F32), "dp")

        proj_sum = whole_sum(proj_grad.reshape(chunks * width, width))
        fc_sum = whole_sum(fc_grad.transpose(1, 0, 2).reshape(width, chunks * width))
        q_sum, k_sum, v_sum, out_sum = (whole_sum(g) for g in (q_grad, k_grad, v_grad, out_w_grad))
    return (
        activations[None],
        tokens_grad[None],
        eight[0],
        eight[1],
        q_sum,
        eight[2],
        k_sum,
        v_sum,
        eight[3],
        out_sum,
        eight[4],
        eight[5],
        eight[6],
        fc_sum,
        fc_bias_sum,
        proj_sum,
        eight[7],
    )


def solution(mesh):
    rows, vec, mat = P("dp", "group", None), P("group"), P("group", None)
    weights = (vec, vec, mat, vec, mat, mat, vec, mat, vec, vec, vec, mat, vec, mat, vec)
    return jax.shard_map(
        partial(on_device, mesh.shape["dp"], mesh.shape["group"]),
        mesh=mesh,
        in_specs=(rows, P("dp", None), rows) + weights,
        out_specs=(rows, rows) + weights,
        check_vma=False,
    )
```

```python
from functools import partial

import jax
import jax.numpy as jnp
from jax import lax
from jax.experimental import pallas as pl
from jax.experimental.pallas import tpu as pltpu
from jax.sharding import PartitionSpec as P

HEAD = 64
LANES = 128
EPSILON = 1e-05
NEG_FILL = -1e30
F32 = jnp.float32
BF16 = jnp.bfloat16
SCALE = HEAD ** (-0.5)


def lane_mask(shape, head):
    lane = lax.broadcasted_iota(jnp.int32, shape, 1)
    return (lane < HEAD) if head == 0 else (lane >= HEAD)


def keep_of(tile_base, tile_len, low_row, own_base):
    span_len = low_row.shape[1]
    key_pos = tile_base + lax.broadcasted_iota(jnp.int32, (tile_len, span_len), 0)
    query_pos = own_base + lax.broadcasted_iota(jnp.int32, (tile_len, span_len), 1)
    return (key_pos >= low_row) & (key_pos <= query_pos)


def tile_loops(bounds_ref, tile, own_tile, tile_count):
    low_tile = bounds_ref[0]
    mid_tile = bounds_ref[1]
    lax.fori_loop(low_tile, mid_tile, lambda t, c: tile(t, True), None)
    lax.fori_loop(mid_tile, own_tile, lambda t, c: tile(t, False), None)
    for t in range(own_tile, tile_count):
        tile(t, True)


def forward_kernel(
    first, pairs, tile_len, last_half, bounds_ref, q_ref, k_ref, v_ref, low_ref, *refs
):
    o_ref, lse_ref, max_ref, sum_ref, acc_ref = refs[-5:]
    span_len = q_ref.shape[0]
    key_len = k_ref.shape[0]
    own_base = key_len - span_len
    last = pl.program_id(0) + first == pairs - 1
    valid = jnp.where(last, last_half, LANES)
    q_t = (q_ref[...].astype(F32) * SCALE).T
    row = lax.broadcasted_iota(jnp.int32, q_t.shape, 0)
    heads = (
        jnp.where(row < HEAD, q_t, 0.0).astype(BF16),
        jnp.where((row >= HEAD) & (row < valid), q_t, 0.0).astype(BF16),
    )
    max_ref[...] = jnp.full_like(max_ref, NEG_FILL)
    sum_ref[...] = jnp.zeros_like(sum_ref)
    acc_ref[...] = jnp.zeros_like(acc_ref)

    def tile(t, masked):
        base = t * tile_len
        rows = pl.ds(pl.multiple_of(base, tile_len), tile_len)
        lane = lax.broadcasted_iota(jnp.int32, (tile_len, LANES), 1)
        k_tile = jnp.where(lane < valid, k_ref[rows, :], jnp.zeros((), BF16))
        v_t = v_ref[rows, :].T
        if masked:
            keep = keep_of(base, tile_len, low_ref[...], own_base)

        def one(head):
            scores = jnp.dot(k_tile, heads[head], preferred_element_type=F32)
            if masked:
                scores = jnp.where(keep, scores, NEG_FILL)
            old_max = max_ref[head]
            new_max = jnp.maximum(old_max, jnp.max(scores, axis=0, keepdims=True))
            shrink = jnp.exp(old_max - new_max)
            probs = jnp.exp(scores - new_max)
            max_ref[head] = new_max
            sum_ref[head] = sum_ref[head] * shrink + jnp.sum(probs, axis=0, keepdims=True)
            acc_ref[head] = acc_ref[head] * shrink + jnp.dot(
                v_t[head * HEAD : (head + 1) * HEAD], probs.astype(BF16), preferred_element_type=F32
            )

        one(0)
        pl.when(valid > HEAD)(lambda: one(1))

    tile_loops(bounds_ref, tile, own_base // tile_len, key_len // tile_len)
    safe = jnp.where(sum_ref[...] > 0, sum_ref[...], 1.0)
    out = jnp.concatenate([acc_ref[0] / safe[0], acc_ref[1] / safe[1]], axis=0)
    o_ref[...] = out.T.astype(BF16)
    lse_ref[0] = jnp.concatenate([max_ref[0] + jnp.log(safe[0]), max_ref[1] + jnp.log(safe[1])], axis=0)


def backward_kernel(
    first, pairs, tile_len, last_half, bounds_ref, q_ref, k_ref, v_ref, g_ref, o_ref, lse_ref, low_ref, *refs
):
    dq_ref, dk_ref, dv_ref, acc_ref = refs[-4:]
    span_len = q_ref.shape[0]
    key_len = k_ref.shape[0]
    own_base = key_len - span_len
    last = pl.program_id(0) + first == pairs - 1
    valid = jnp.where(last, last_half, LANES)
    lane = lax.broadcasted_iota(jnp.int32, (span_len, LANES), 1)
    q_now = jnp.where(lane < valid, q_ref[...].astype(F32) * SCALE, 0.0)
    g_now = jnp.where(lane < valid, g_ref[...].astype(F32), 0.0)
    o_now = jnp.where(lane < valid, o_ref[...].astype(F32), 0.0)
    q_t, g_t, o_t = q_now.T, g_now.T, o_now.T
    row = lax.broadcasted_iota(jnp.int32, q_t.shape, 0)
    prod = g_t * o_t
    part = []
    for head in range(2):
        row_ok = (row < HEAD) if head == 0 else (row >= HEAD)
        lane_ok = (lane < HEAD) if head == 0 else (lane >= HEAD)
        part.append(
            (
                jnp.where(row_ok, q_t, 0.0).astype(BF16),
                jnp.where(row_ok, g_t, 0.0).astype(BF16),
                jnp.where(lane_ok, q_now, 0.0).astype(BF16),
                jnp.where(lane_ok, g_now, 0.0).astype(BF16),
                jnp.sum(prod[head * HEAD : (head + 1) * HEAD], axis=0, keepdims=True),
                lse_ref[0, head : head + 1],
            )
        )
    acc_ref[...] = jnp.zeros_like(acc_ref)

    def clear(t, carry):
        rows = pl.ds(pl.multiple_of(t * tile_len, tile_len), tile_len)
        dk_ref[rows, :] = jnp.zeros((tile_len, LANES), BF16)
        dv_ref[rows, :] = jnp.zeros((tile_len, LANES), BF16)
        return carry

    lax.fori_loop(0, bounds_ref[0], clear, None)

    def tile(t, masked):
        base = t * tile_len
        rows = pl.ds(pl.multiple_of(base, tile_len), tile_len)
        lane_k = lax.broadcasted_iota(jnp.int32, (tile_len, LANES), 1)
        k_tile = jnp.where(lane_k < valid, k_ref[rows, :], jnp.zeros((), BF16))
        v_tile = jnp.where(lane_k < valid, v_ref[rows, :], jnp.zeros((), BF16))
        k_t = k_tile.T
        if masked:
            keep = keep_of(base, tile_len, low_ref[...], own_base)

        def one(head):
            qh_t, gh_t, qh, gh, delta, lse = part[head]
            scores = jnp.dot(k_tile, qh_t, preferred_element_type=F32)
            probs = jnp.exp(scores - lse)
            if masked:
                probs = jnp.where(keep, probs, 0.0)
            dprobs = jnp.dot(v_tile, gh_t, preferred_element_type=F32)
            dscores = (probs * (dprobs - delta)).astype(BF16)
            dv = jnp.dot(probs.astype(BF16), gh, preferred_element_type=F32)
            dk = jnp.dot(dscores, qh, preferred_element_type=F32)
            acc_ref[head] += jnp.dot(
                k_t[head * HEAD : (head + 1) * HEAD], dscores, preferred_element_type=F32
            )
            return dk, dv

        def write(dk, dv):
            dk_ref[rows, :] = dk.astype(BF16)
            dv_ref[rows, :] = dv.astype(BF16)

        @pl.when(valid > HEAD)
        def _():
            dk_a, dv_a = one(0)
            dk_b, dv_b = one(1)
            write(dk_a + dk_b, dv_a + dv_b)

        @pl.when(valid <= HEAD)
        def _():
            write(*one(0))

    tile_loops(bounds_ref, tile, own_base // tile_len, key_len // tile_len)
    dq_ref[...] = (jnp.concatenate([acc_ref[0], acc_ref[1]], axis=0).T * SCALE).astype(BF16)


def attend_parts(pairs, number):
    size = pl.cdiv(pairs, number)
    return [(first, min(size, pairs - first)) for first in range(0, pairs, size)]


def attend_specs(first, span_len, key_len):
    own = pl.BlockSpec((span_len, LANES), lambda p, b: (0, p + first))
    keys = pl.BlockSpec((key_len, LANES), lambda p, b: (0, p + first))
    low = pl.BlockSpec((1, span_len), lambda p, b: (0, 0))
    lse = pl.BlockSpec((1, 2, span_len), lambda p, b: (p + first, 0, 0))
    return own, keys, low, lse


def attend_call(kernel, name, part, span_len, key_len, width, inputs, in_kinds, outs, out_kinds, earlier, scratch, flops):
    first, number = part
    pairs = pl.cdiv(width, LANES)
    tile_len = 256 if span_len % 256 == 0 else span_len
    last_half = width - (pairs - 1) * LANES
    specs = dict(zip(("own", "keys", "low", "lse"), attend_specs(first, span_len, key_len)))
    earlier = () if earlier is None else tuple(earlier)
    return pl.pallas_call(
        partial(kernel, first, pairs, tile_len, last_half),
        out_shape=outs,
        grid_spec=pltpu.PrefetchScalarGridSpec(
            num_scalar_prefetch=1,
            grid=(number,),
            in_specs=[specs[kind] for kind in in_kinds] + [pl.BlockSpec(memory_space=pl.ANY)] * len(earlier),
            out_specs=tuple(specs[kind] for kind in out_kinds),
            scratch_shapes=scratch,
        ),
        input_output_aliases={len(inputs) + i: i for i in range(len(earlier))},
        cost_estimate=pl.CostEstimate(flops=flops * span_len * LANES, bytes_accessed=span_len * width, transcendentals=0),
        compiler_params=pltpu.CompilerParams(vmem_limit_bytes=40 * 1024 * 1024),
        name=name,
    )(*inputs, *earlier)


def attend_forward(part, queries, keys, values, low_row, bounds, earlier=None):
    span_len, width = queries.shape
    key_len = keys.shape[0]
    return attend_call(
        forward_kernel,
        "attend_forward",
        part,
        span_len,
        key_len,
        width,
        (bounds, queries, keys, values, low_row),
        ("own", "keys", "keys", "low"),
        (
            jax.ShapeDtypeStruct((span_len, width), BF16),
            jax.ShapeDtypeStruct((pl.cdiv(width, LANES), 2, span_len), F32),
        ),
        ("own", "lse"),
        earlier,
        [
            pltpu.VMEM((2, 1, span_len), F32),
            pltpu.VMEM((2, 1, span_len), F32),
            pltpu.VMEM((2, HEAD, span_len), F32),
        ],
        16,
    )


def attend_backward(part, queries, keys, values, out_grad, attended, lse, low_row, bounds, earlier=None):
    span_len, width = queries.shape
    key_len = keys.shape[0]
    return attend_call(
        backward_kernel,
        "attend_backward",
        part,
        span_len,
        key_len,
        width,
        (bounds, queries, keys, values, out_grad, attended, lse, low_row),
        ("own", "keys", "keys", "own", "own", "lse", "low"),
        (
            jax.ShapeDtypeStruct((span_len, width), BF16),
            jax.ShapeDtypeStruct((key_len, width), BF16),
            jax.ShapeDtypeStruct((key_len, width), BF16),
        ),
        ("own", "keys", "keys"),
        earlier,
        [pltpu.VMEM((2, HEAD, span_len), F32)],
        40,
    )


def along_group(x, step, count, wrap):
    pairs = [(i, (i + step) % count) for i in range(count) if wrap or 0 <= i + step < count]
    return lax.ppermute(x, "group", pairs)


def flip(x, bit, count):
    return lax.ppermute(x, "dp", [(i, i ^ bit) for i in range(count)])


CORE, ACROSS, DOWN = 1, 2, 4


def pick(x, index, axis=0):
    return lax.dynamic_index_in_dim(x, index, axis, keepdims=False)


def put(x, part, index):
    start = tuple(index) + (0,) * (x.ndim - len(index))
    part = part.reshape((1,) * len(index) + part.shape)
    return lax.dynamic_update_slice(x, part, start)


def after(x, *before):
    return lax.optimization_barrier((x,) + before)[0]


def plane_share_near(mine, count):
    return flip(mine, ACROSS, count), flip(mine, DOWN, count)


def plane_share_far(from_x, from_y, count):
    cut = cut_of(from_x)
    return flip(from_x[:, :cut], DOWN, count), flip(from_y[:, cut:], ACROSS, count)


def cut_of(part):
    return (part.shape[1] // 2 + 7) // 8 * 8


def assemble_kernel(groups, kind, here_ref, own_ref, *refs):
    sources, outs, sems = refs[:10], refs[10:-1], refs[-1]
    chip, core, z = here_ref[0], here_ref[1], here_ref[2]
    cut = sources[3].shape[1]

    def place(index, plane, half):
        if kind == "plane":
            return outs[0].at[plane, index, half]
        if kind == "chip":
            return outs[0].at[index, plane, half]
        return outs[index].at[plane, half]

    def move(index, k, wait):
        n = 1 + k * 2 * (groups - 1)
        for side in range(2):
            half = core if side == 0 else 1 - core
            for step in range(groups - 1):
                target = place(index, lax.rem(z - step - 1 + groups, groups), half)
                if k < 3:
                    pairs = [(sources[side * 5 + k].at[step], target)]
                else:
                    pairs = [
                        (sources[side * 5 + 3].at[step], target.at[:cut]),
                        (sources[side * 5 + 4].at[step], target.at[cut:]),
                    ]
                for src, dst in pairs:
                    copy = pltpu.make_async_copy(src, dst, sems.at[n])
                    copy.wait() if wait else copy.start()
                    n += 1

    if kind == "plane":
        owns = [(own_ref, outs[0].at[z])]
    elif kind == "chip":
        owns = [(own_ref, outs[0].at[:, z])]
    else:
        owns = [(own_ref.at[m], outs[m].at[z]) for m in range(4)]
    last = sems.shape[0] - len(owns)
    owns = [pltpu.make_async_copy(src, dst, sems.at[last + i]) for i, (src, dst) in enumerate(owns)]
    for copy in owns:
        copy.start()
    for wait in (False, True):
        for k in range(4):
            if kind == "apart":
                for m in range(4):
                    pl.when(chip == m ^ k)(partial(move, m, k, wait))
            else:
                move(chip ^ k, k, wait)
    for copy in owns:
        copy.wait()


def assemble(own, sources, here, groups, kind):
    rows, cols = own.shape[2:]
    if kind == "apart":
        shapes = [(groups, 2, rows, cols)] * 4
    else:
        shapes = [(groups, 4, 2, rows, cols) if kind == "plane" else (4, groups, 2, rows, cols)]
    return pl.pallas_call(
        partial(assemble_kernel, groups, kind),
        out_shape=[jax.ShapeDtypeStruct(shape, own.dtype) for shape in shapes],
        grid_spec=pltpu.PrefetchScalarGridSpec(
            num_scalar_prefetch=1,
            grid=(1,),
            in_specs=[pl.BlockSpec(memory_space=pl.ANY)] * 11,
            out_specs=[pl.BlockSpec(shape, lambda i, h, n=len(shape): (0,) * n) for shape in shapes],
            scratch_shapes=[pltpu.SemaphoreType.DMA((1 + 10 * (groups - 1) + 4,))],
        ),
        compiler_params=pltpu.CompilerParams(vmem_limit_bytes=40 * 1024 * 1024),
        cost_estimate=pl.CostEstimate(flops=0, bytes_accessed=own.size, transcendentals=0),
        name="assemble",
    )(jnp.stack(here).astype(jnp.int32), own, *sources)


def from_planes(piece, groups):
    return jnp.stack([along_group(piece, step, groups, True) for step in range(1, groups)])


def chip_sum(parts, core, count, axis):
    got = flip(pick(parts, 1 - core, axis), CORE, count)
    return (pick(parts, core, axis).astype(F32) + got.astype(F32)).astype(BF16)


def plane_first_step(half, chip, count, axis):
    to_diag = pick(half, chip ^ 3, axis)
    cut = to_diag.shape[0] // 2
    return flip(to_diag[:cut], ACROSS, count), flip(to_diag[cut:], DOWN, count)


def plane_second_step(half, via, chip, count, axis):
    to_own, to_x, to_y = (pick(half, chip ^ k, axis) for k in range(3))
    cut = to_own.shape[0] // 2
    from_y = flip(jnp.concatenate([to_y[:cut] + via[0], to_y[cut:]]), DOWN, count)
    from_x = flip(jnp.concatenate([to_x[:cut], to_x[cut:] + via[1]]), ACROSS, count)
    return (to_own.astype(F32) + from_x.astype(F32) + from_y.astype(F32)).astype(BF16)


def line_sum(mine, z, groups):
    total = pick(mine, z).astype(F32)
    for step in range(1, groups):
        sent = pick(mine, lax.rem(z + step, groups))
        total = total + along_group(sent, step, groups, True).astype(F32)
    return total


def shares_of(mine, near, far):
    return jnp.concatenate((mine,) + near + (jnp.concatenate(far, axis=1),))


def core_copies(shares, chip, core, count):
    other = flip(shares, CORE, count)
    out = jnp.zeros((4, 2) + shares.shape[1:], shares.dtype)
    for k in range(4):
        out = put(out, shares[k], (chip ^ k, core))
        out = put(out, other[k], (chip ^ k, 1 - core))
    return out


def mean_spread(values):
    center = values - jnp.mean(values, axis=-1, keepdims=True)
    spread = jnp.mean(center * center, axis=-1, keepdims=True)
    return center, lax.rsqrt(spread + EPSILON)


def layer_norm(values, gain, shift):
    center, scale = mean_spread(values)
    return center * scale * gain + shift


def layer_norm_back(values, gain, grad):
    center, scale = mean_spread(values)
    unit = center * scale
    inner = grad * gain
    back = scale * (
        inner
        - jnp.mean(inner, axis=-1, keepdims=True)
        - unit * jnp.mean(inner * unit, axis=-1, keepdims=True)
    )
    return back, jnp.sum(grad * unit, axis=0), jnp.sum(grad, axis=0)


def row_sum(values):
    return jnp.sum(values.astype(F32), axis=0)


def matmul(left, right):
    return jnp.dot(left, right, preferred_element_type=F32)


def weight_grad(left, right):
    return jnp.einsum("ra,rb->ab", left, right, preferred_element_type=F32).astype(BF16)


def back_through(grad_rows, weight):
    return jnp.einsum("rb,ab->ra", grad_rows, weight, preferred_element_type=F32)


def on_device(
    count,
    groups,
    tokens,
    segments,
    out_grad,
    norm1_gain,
    norm1_bias,
    w_query,
    query_bias,
    w_key,
    w_value,
    value_bias,
    w_out,
    out_bias,
    norm2_gain,
    norm2_bias,
    w_fc,
    fc_bias,
    w_proj,
    proj_bias,
):
    _, span_len, width = tokens.shape
    shard = width // groups
    half = shard // 2
    chunks = w_fc.shape[1] // width
    key_len = segments.shape[1]
    z = lax.axis_index("group")
    place = lax.axis_index("dp")
    fast = count == 8 and groups == 4 and chunks == 4
    chip, core = place // 2, lax.rem(place, 2)
    here = (chip, core, z)
    forward_parts = attend_parts(pl.cdiv(width, LANES), 3)
    parts = attend_parts(pl.cdiv(width, LANES), 5)

    small = jnp.concatenate(
        [norm1_gain, norm1_bias, query_bias, value_bias, out_bias, norm2_gain, norm2_bias, proj_bias, fc_bias]
    )
    small_rel = jnp.stack([small] + [along_group(small, step, groups, True) for step in range(1, groups)])
    small_all = jnp.take(small_rel, lax.rem(z - jnp.arange(groups) + groups, groups), axis=0)
    vectors = small_all[:, : 8 * shard].reshape(groups, 8, shard).transpose(1, 0, 2).reshape(8, width)
    gain_one, shift_one, bias_q, bias_v, bias_o, gain_two, shift_two, bias_p = vectors.astype(F32)
    bias_fc = small_all[:, 8 * shard :].astype(F32).reshape(chunks, 1, width)

    mine = tokens[0]
    inputs = mine.astype(F32)
    normed_one = layer_norm(inputs, gain_one, shift_one).astype(BF16)
    own_base = key_len - span_len
    if fast:
        attn_own = jnp.stack([w_query, w_key, w_value, w_out]).reshape(4, 2, half, width)
        attn_ring = from_planes(pick(pick(attn_own, chip), core), groups)
        attn_near = plane_share_near(attn_ring, count)
        hops = [mine, along_group(after(mine, attn_ring), 1, groups, False)]
        attn_three = (attn_ring,) + attn_near
        attn_far = plane_share_far(*attn_near, count)
        attn_other = tuple(flip(after(part, *attn_near), CORE, count) for part in attn_three)
        attn_other += tuple(flip(after(part, hops[1]), CORE, count) for part in attn_far)
        hops.append(along_group(after(hops[1], *attn_far), 1, groups, False))
        attn = assemble(attn_own, attn_three + attn_far + attn_other, here, groups, "apart")
        full_q, full_k, full_v, full_o = (part.reshape(width, width) for part in attn)
        queries = (matmul(normed_one, full_q) + bias_q).astype(BF16)
        fc_own = w_fc.reshape(2, half, chunks, width).transpose(2, 0, 1, 3)
        fc_piece = pick(pick(fc_own, chip), core)
        proj_own = w_proj.reshape(4, 2, half, width)
        proj_piece = pick(pick(proj_own, chip), core)
        hops.append(along_group(after(hops[2], queries), 1, groups, False))
        fc_ring = from_planes(after(fc_piece, hops[3]), groups)
    else:
        gather = partial(lax.all_gather, axis_name="group", axis=0, tiled=True)
        full_q, full_k, full_v, full_o = (gather(w) for w in (w_query, w_key, w_value, w_out))
        full_fc = gather(w_fc).reshape(width, chunks, width).transpose(1, 0, 2)
        full_proj = gather(w_proj).reshape(chunks, width, width)
        queries = (matmul(normed_one, full_q) + bias_q).astype(BF16)
        hops = [mine]
        for _ in range(groups - 1):
            hops.append(along_group(hops[-1], 1, groups, False))
    reach = jnp.concatenate(hops[::-1]).astype(F32)

    seg = segments[0]
    seg_mine = lax.dynamic_slice_in_dim(seg, z * span_len, span_len)
    low_row = jnp.sum((seg[None, :] < seg_mine[:, None]).astype(jnp.int32), axis=1)
    low_row = low_row + (groups - 1 - z) * span_len
    tile_len = 256 if span_len % 256 == 0 else span_len
    low_tile = low_row[0] // tile_len
    mid_tile = jnp.clip((low_row[-1] + tile_len - 1) // tile_len, low_tile, own_base // tile_len)
    bounds = jnp.stack([low_tile, mid_tile]).astype(jnp.int32)
    low_row = low_row[None]

    normed_all = layer_norm(reach, gain_one, shift_one).astype(BF16)
    keys = matmul(normed_all, full_k).astype(BF16)
    values = (matmul(normed_all, full_v) + bias_v).astype(BF16)
    state = None
    for number, part in enumerate(forward_parts):
        row_now = low_row
        if fast and number == 1:
            fc_near = plane_share_near(after(fc_ring, state[0]), count)
            proj_ring = from_planes(after(proj_piece, fc_ring, state[0]), groups)
            row_now = after(low_row, fc_ring)
        if fast and number == 2:
            fc_three = (fc_ring,) + fc_near
            fc_far = plane_share_far(*(after(part, state[0]) for part in fc_near), count)
            fc_other = tuple(flip(after(part, state[0], *fc_near), CORE, count) for part in fc_three)
            row_now = after(low_row, *fc_near)
        state = attend_forward(part, queries, keys, values, row_now, bounds, state)
    attended, lse = state
    if fast:
        fc_other += tuple(flip(after(part, attended), CORE, count) for part in fc_far)
        proj_near = plane_share_near(after(proj_ring, attended, *fc_far), count)
        attended = after(attended, proj_ring, *fc_far)
    resid = inputs + matmul(attended, full_o) + bias_o
    normed_two = layer_norm(resid, gain_two, shift_two).astype(BF16)
    if fast:
        full_fc = assemble(after(fc_own, normed_two), fc_three + fc_far + fc_other, here, groups, "chip")
        full_fc = full_fc[0].reshape(4, width, width)
    pre_act = jnp.einsum("td,jdf->jtf", normed_two, full_fc, preferred_element_type=F32) + bias_fc
    gelu_tanh = partial(jax.nn.gelu, approximate=True)
    hidden, gelu_back = jax.vjp(gelu_tanh, pre_act)
    hidden = hidden.astype(BF16)

    cot = out_grad[0]
    proj_bias_grad = row_sum(cot)
    cot_now = cot
    if fast:
        proj_three = (proj_ring,) + proj_near
        proj_far = plane_share_far(*(after(part, hidden) for part in proj_near), count)
        proj_other = tuple(flip(after(part, hidden, *proj_near), CORE, count) for part in proj_three)
        cot_now = after(cot, *proj_near)
    proj_grad = jnp.einsum("jtf,td->jfd", hidden, cot_now, preferred_element_type=F32).astype(BF16)
    cot_now = after(cot, proj_grad)
    if fast:
        proj_chip = chip_sum(proj_grad.reshape(groups, 4, 2, half, width), core, count, 2)
        proj_other += tuple(flip(after(part, proj_grad), CORE, count) for part in proj_far)
        full_proj = assemble(proj_own, proj_three + proj_far + proj_other, here, groups, "plane")
        full_proj = full_proj[0].reshape(4, width, width)
        proj_via = plane_first_step(proj_chip, chip, count, 1)
        cot_now = after(cot, proj_chip)
    hidden_grad = jnp.einsum("td,jfd->jtf", cot_now, full_proj, preferred_element_type=F32)
    pre_grad = gelu_back(hidden_grad)[0].astype(BF16)
    fc_bias_grad = jnp.sum(pre_grad.astype(F32), axis=1)
    normed_two_now = after(normed_two, *proj_via) if fast else normed_two
    fc_grad = jnp.einsum("td,jtf->jdf", normed_two_now, pre_grad, preferred_element_type=F32).astype(BF16)
    normed_two_grad = jnp.einsum("jtf,jdf->td", after(pre_grad, fc_grad), full_fc, preferred_element_type=F32)
    resid_part, gain_two_grad, shift_two_grad = layer_norm_back(resid, gain_two, normed_two_grad)
    resid_grad = cot.astype(F32) + resid_part
    resid_low = resid_grad.astype(BF16)
    out_bias_grad = row_sum(resid_low)
    attended_grad = back_through(resid_low, full_o).astype(BF16)
    out_w_grad = weight_grad(attended, resid_low)
    if fast:
        proj_mine = plane_second_step(after(proj_chip, pre_grad), proj_via, chip, count, 1)
        fc_chip = chip_sum(fc_grad.reshape(4, groups, 2, half, width), core, count, 2)
        fc_via = plane_first_step(after(fc_chip, proj_mine, attended_grad), chip, count, 0)
        proj_line = line_sum(after(proj_mine, attended_grad), z, groups).astype(BF16)
    state = None
    for number, part in enumerate(parts):
        row_now = low_row
        if fast and number == 0:
            row_now = after(low_row, proj_mine, fc_chip)
        if fast and number == 1:
            fc_mine = plane_second_step(after(fc_chip, state[0]), fc_via, chip, count, 0)
            row_now = after(low_row, *fc_via)
        if fast and number == 2:
            proj_line_near = plane_share_near(after(proj_line, state[0])[None], count)
            row_now = after(low_row, proj_line)
        if fast and number == 3:
            proj_line_far = plane_share_far(*(after(part, state[0]) for part in proj_line_near), count)
            fc_line = line_sum(after(fc_mine, state[0]), z, groups).astype(BF16)
            row_now = after(low_row, fc_mine, *proj_line_near)
        if fast and number == 4:
            proj_shares = shares_of(after(proj_line, state[0])[None], proj_line_near, proj_line_far)
            proj_copies = core_copies(proj_shares, chip, core, count)
            row_now = after(low_row, *proj_line_far)
        state = attend_backward(part, queries, keys, values, attended_grad, attended, lse, row_now, bounds, state)
    dqueries, dkeys, dvalues = state
    query_bias_grad = row_sum(dqueries)
    value_bias_grad = row_sum(dvalues)
    if fast:
        fc_line_near = plane_share_near(after(fc_line, dkeys)[None], count)
    norm_terms = back_through(dkeys, full_k) + back_through(dvalues, full_v)
    moving = None
    for step in range(groups - 1):
        term = norm_terms[step * span_len : (step + 1) * span_len]
        if moving is not None:
            term = term + moving.astype(F32)
        moving = along_group(term.astype(BF16), -1, groups, False)
    normed_now = after(normed_all, norm_terms)
    if fast:
        normed_now = after(normed_now, *fc_line_near)
        fc_line_far = plane_share_far(*(after(part, norm_terms) for part in fc_line_near), count)
        fc_shares = shares_of(fc_line[None], fc_line_near, fc_line_far)
        fc_copies = core_copies(fc_shares, chip, core, count)
    q_grad = weight_grad(normed_one, dqueries)
    k_grad = weight_grad(normed_now, dkeys)
    v_grad = weight_grad(normed_now, dvalues)
    hidden_now = hidden
    if fast:
        attn_grads = jnp.stack([q_grad, k_grad, v_grad, out_w_grad]).reshape(4, groups, 2, half, width)
        attn_chip = chip_sum(attn_grads, core, count, 2)
        attn_via = plane_first_step(attn_chip, chip, count, 0)
        hidden_now = after(hidden, attn_chip)
        attn_mine = plane_second_step(attn_chip, attn_via, chip, count, 0)
        attn_line = line_sum(attn_mine, z, groups).astype(BF16)
        attn_near = plane_share_near(attn_line[None], count)
        attn_far = plane_share_far(*attn_near, count)
        attn_sum = core_copies(shares_of(attn_line[None], attn_near, attn_far), chip, core, count)
    activations = resid + jnp.einsum("jtf,jfd->td", hidden_now, full_proj, preferred_element_type=F32) + bias_p
    normed_one_grad = back_through(dqueries, full_q) + norm_terms[own_base:] + moving.astype(F32)
    input_part, gain_one_grad, shift_one_grad = layer_norm_back(inputs, gain_one, normed_one_grad)
    tokens_grad = resid_grad + input_part

    vector_grads = jnp.stack(
        [
            gain_one_grad,
            shift_one_grad,
            query_bias_grad,
            value_bias_grad,
            out_bias_grad,
            gain_two_grad,
            shift_two_grad,
            proj_bias_grad,
        ]
    )
    vector_grads = vector_grads.reshape(8, groups, shard).transpose(1, 0, 2).reshape(groups, 8 * shard)
    vector_grads = jnp.concatenate([vector_grads, fc_bias_grad.reshape(groups, -1)], axis=1)
    bit = 1
    while bit < count:
        vector_grads = vector_grads + flip(vector_grads, bit, count)
        bit *= 2
    vector_sums = line_sum(vector_grads, z, groups)
    eight = vector_sums[: 8 * shard].reshape(8, shard)
    fc_bias_sum = vector_sums[8 * shard :]
    if fast:
        attn_sum = attn_sum.reshape(4, shard, width).astype(F32)
        proj_sum = proj_copies.reshape(4 * shard, width).astype(F32)
        fc_sum = fc_copies.reshape(4, shard, width).transpose(1, 0, 2).reshape(shard, 4 * width).astype(F32)
        q_sum, k_sum, v_sum, out_sum = attn_sum[0], attn_sum[1], attn_sum[2], attn_sum[3]
    else:

        def whole_sum(part):
            part = lax.psum_scatter(part, "group", scatter_dimension=0, tiled=True)
            return lax.psum(part.astype(F32), "dp")

        proj_sum = whole_sum(proj_grad.reshape(chunks * width, width))
        fc_sum = whole_sum(fc_grad.transpose(1, 0, 2).reshape(width, chunks * width))
        q_sum, k_sum, v_sum, out_sum = (whole_sum(g) for g in (q_grad, k_grad, v_grad, out_w_grad))
    return (
        activations[None],
        tokens_grad[None],
        eight[0],
        eight[1],
        q_sum,
        eight[2],
        k_sum,
        v_sum,
        eight[3],
        out_sum,
        eight[4],
        eight[5],
        eight[6],
        fc_sum,
        fc_bias_sum,
        proj_sum,
        eight[7],
    )


def solution(mesh):
    rows, vec, mat = P("dp", "group", None), P("group"), P("group", None)
    weights = (vec, vec, mat, vec, mat, mat, vec, mat, vec, vec, vec, mat, vec, mat, vec)
    return jax.shard_map(
        partial(on_device, mesh.shape["dp"], mesh.shape["group"]),
        mesh=mesh,
        in_specs=(rows, P("dp", None), rows) + weights,
        out_specs=(rows, rows) + weights,
        check_vma=False,
    )
```

```python
from functools import partial

import jax
import jax.numpy as jnp
from jax import lax
from jax.experimental import pallas as pl
from jax.experimental.pallas import tpu as pltpu
from jax.sharding import PartitionSpec as P

HEAD = 64
LANES = 128
EPSILON = 1e-05
NEG_FILL = -1e30
F32 = jnp.float32
BF16 = jnp.bfloat16
SCALE = HEAD ** (-0.5)
VMEM_BYTES = 40 * 1024 * 1024
ATTEND_BYTES = 20 * 1024 * 1024


def tile_length(span_len):
    return 256 if span_len % 256 == 0 else span_len


def keep_of(tile_base, tile_len, low_row, own_base):
    span_len = low_row.shape[1]
    key_pos = tile_base + lax.broadcasted_iota(jnp.int32, (tile_len, span_len), 0)
    query_pos = own_base + lax.broadcasted_iota(jnp.int32, (tile_len, span_len), 1)
    return (key_pos >= low_row) & (key_pos <= query_pos)


def tile_loops(bounds_ref, tile, base_tile, count, own_tile):
    low_tile = bounds_ref[0]
    mid_tile = bounds_ref[1]
    clear_end = min(max(own_tile - base_tile, 0), count)
    begin = jnp.clip(low_tile - base_tile, 0, clear_end)
    middle = jnp.clip(mid_tile - base_tile, begin, clear_end)
    lax.fori_loop(begin, middle, lambda t, c: tile(t, True), None)
    lax.fori_loop(middle, clear_end, lambda t, c: tile(t, False), None)
    for t in range(clear_end, count):
        tile(t, True)
    return begin


def inside(x, axis, valid):
    where = lax.broadcasted_iota(jnp.int32, x.shape, axis)
    return jnp.where(where < valid, x, jnp.zeros((), x.dtype))


def halves(x, axis):
    where = lax.broadcasted_iota(jnp.int32, x.shape, axis)
    zero = jnp.zeros((), x.dtype)
    return jnp.where(where < HEAD, x, zero), jnp.where(where >= HEAD, x, zero)


def forward_kernel(first, pairs, last_half, lengths, bounds_ref, qt_ref, low_ref, *refs):
    blocks = len(lengths)
    k_refs, v_refs = refs[:blocks], refs[blocks : 2 * blocks]
    ot_ref, lse_ref, max_ref, sum_ref, acc_ref = refs[-5:]
    span_len = qt_ref.shape[1]
    tile_len = tile_length(span_len)
    own_base = sum(lengths) - span_len
    last = pl.program_id(0) + first == pairs - 1
    valid = jnp.where(last, last_half, LANES)
    heads = halves(inside((qt_ref[...].astype(F32) * SCALE).astype(BF16), 0, valid), 0)
    max_ref[...] = jnp.full_like(max_ref, NEG_FILL)
    sum_ref[...] = jnp.zeros_like(sum_ref)
    acc_ref[...] = jnp.zeros_like(acc_ref)
    base = 0
    for k_ref, v_ref, length in zip(k_refs, v_refs, lengths):

        def tile(t, masked, k_ref=k_ref, v_ref=v_ref, base=base):
            rows = pl.ds(pl.multiple_of(t * tile_len, tile_len), tile_len)
            k_tile = inside(k_ref[rows, :], 1, valid)
            v_t = v_ref[rows, :].T
            if masked:
                keep = keep_of(base + t * tile_len, tile_len, low_ref[...], own_base)

            def one(head):
                scores = jnp.dot(k_tile, heads[head], preferred_element_type=F32)
                if masked:
                    scores = jnp.where(keep, scores, NEG_FILL)
                old_max = max_ref[head]
                new_max = jnp.maximum(old_max, jnp.max(scores, axis=0, keepdims=True))
                shrink = jnp.exp(old_max - new_max)
                probs = jnp.exp(scores - new_max)
                max_ref[head] = new_max
                sum_ref[head] = sum_ref[head] * shrink + jnp.sum(probs, axis=0, keepdims=True)
                acc_ref[head] = acc_ref[head] * shrink + jnp.dot(
                    v_t[head * HEAD : (head + 1) * HEAD], probs.astype(BF16), preferred_element_type=F32
                )

            @pl.when(valid > HEAD)
            def _():
                one(0)
                one(1)

            @pl.when(valid <= HEAD)
            def _():
                one(0)

        tile_loops(bounds_ref, tile, base // tile_len, length // tile_len, own_base // tile_len)
        base += length
    safe = jnp.where(sum_ref[...] > 0, sum_ref[...], 1.0)
    ot_ref[...] = jnp.concatenate([acc_ref[0] / safe[0], acc_ref[1] / safe[1]], axis=0).astype(BF16)
    lse_ref[0] = jnp.concatenate([max_ref[0] + jnp.log(safe[0]), max_ref[1] + jnp.log(safe[1])], axis=0)


def backward_kernel(
    base, final, pairs, last_half, own_base, bounds_ref, q_ref, qt_ref, g_ref, gt_ref, ot_ref, lse_ref, low_ref, k_ref, v_ref, *refs
):
    first = base == 0
    acc_in = None if first else refs[0]
    acc_out, dk_ref, dv_ref, sums_ref, acc_ref = refs[-5:]
    span_len = q_ref.shape[0]
    tile_len = tile_length(span_len)
    last = pl.program_id(0) == pairs - 1
    valid = jnp.where(last, last_half, LANES)
    q_heads = halves(inside((q_ref[...].astype(F32) * SCALE).astype(BF16), 1, valid), 1)
    qt_heads = halves(inside((qt_ref[...].astype(F32) * SCALE).astype(BF16), 0, valid), 0)
    g_heads = halves(inside(g_ref[...], 1, valid), 1)
    gt_now = inside(gt_ref[...], 0, valid)
    gt_heads = halves(gt_now, 0)
    prod = gt_now.astype(F32) * inside(ot_ref[...], 0, valid).astype(F32)
    deltas = [jnp.sum(prod[h * HEAD : (h + 1) * HEAD], axis=0, keepdims=True) for h in range(2)]
    if first:
        acc_ref[...] = jnp.zeros_like(acc_ref)
    else:
        acc_ref[...] = acc_in[0]

    def tile(t, masked):
        rows = pl.ds(pl.multiple_of(t * tile_len, tile_len), tile_len)
        k_tile = inside(k_ref[rows, :], 1, valid)
        v_tile = inside(v_ref[rows, :], 1, valid)
        k_t = k_tile.T
        if masked:
            keep = keep_of(base + t * tile_len, tile_len, low_ref[...], own_base)

        def one(head):
            scores = jnp.dot(k_tile, qt_heads[head], preferred_element_type=F32)
            probs = jnp.exp(scores - lse_ref[0, head : head + 1])
            if masked:
                probs = jnp.where(keep, probs, 0.0)
            dprobs = jnp.dot(v_tile, gt_heads[head], preferred_element_type=F32)
            dscores = (probs * (dprobs - deltas[head])).astype(BF16)
            dv = jnp.dot(probs.astype(BF16), g_heads[head], preferred_element_type=F32)
            dk = jnp.dot(dscores, q_heads[head], preferred_element_type=F32)
            acc_ref[head] += jnp.dot(k_t[head * HEAD : (head + 1) * HEAD], dscores, preferred_element_type=F32)
            return dk, dv

        def write(dk, dv):
            dk_ref[rows, :] = dk.astype(BF16)
            dv_ref[rows, :] = dv.astype(BF16)

        @pl.when(valid > HEAD)
        def _():
            dk_a, dv_a = one(0)
            dk_b, dv_b = one(1)
            write(dk_a + dk_b, dv_a + dv_b)

        @pl.when(valid <= HEAD)
        def _():
            write(*one(0))

    begin = tile_loops(bounds_ref, tile, base // tile_len, k_ref.shape[0] // tile_len, own_base // tile_len)

    def clear(t, carry):
        rows = pl.ds(pl.multiple_of(t * tile_len, tile_len), tile_len)
        dk_ref[rows, :] = jnp.zeros((tile_len, LANES), BF16)
        dv_ref[rows, :] = jnp.zeros((tile_len, LANES), BF16)
        return carry

    lax.fori_loop(0, begin, clear, None)
    dv_sum = jnp.sum(dv_ref[...].astype(F32), axis=0, keepdims=True)
    if final:
        dq = (jnp.concatenate([acc_ref[0], acc_ref[1]], axis=0).T * SCALE).astype(BF16)
        acc_out[...] = dq
        sums_ref[...] = jnp.concatenate([dv_sum, jnp.sum(dq.astype(F32), axis=0, keepdims=True)], axis=0)
    else:
        acc_out[0] = acc_ref[...]
        sums_ref[...] = jnp.concatenate([dv_sum, jnp.zeros_like(dv_sum)], axis=0)


def attend_parts(pairs, number):
    size = pl.cdiv(pairs, number)
    return [(first, min(size, pairs - first)) for first in range(0, pairs, size)]


def attend_forward(part, queries_t, keys, values, low_row, bounds, earlier):
    first, number = part
    width, span_len = queries_t.shape
    pairs = pl.cdiv(width, LANES)
    lengths = tuple(block.shape[0] for block in keys)
    turned = pl.BlockSpec((LANES, span_len), lambda p, b: (p + first, 0))
    low_spec = pl.BlockSpec((1, span_len), lambda p, b: (0, 0))
    key_specs = [pl.BlockSpec((length, LANES), lambda p, b: (0, p + first)) for length in lengths]
    lse_spec = pl.BlockSpec((1, 2, span_len), lambda p, b: (p + first, 0, 0))
    inputs = (bounds, queries_t, low_row) + tuple(keys) + tuple(values)
    earlier = () if earlier is None else tuple(earlier)
    return pl.pallas_call(
        partial(forward_kernel, first, pairs, width - (pairs - 1) * LANES, lengths),
        out_shape=(
            jax.ShapeDtypeStruct((width, span_len), BF16),
            jax.ShapeDtypeStruct((pairs, 2, span_len), F32),
        ),
        grid_spec=pltpu.PrefetchScalarGridSpec(
            num_scalar_prefetch=1,
            grid=(number,),
            in_specs=[turned, low_spec] + key_specs + key_specs + [pl.BlockSpec(memory_space=pl.ANY)] * len(earlier),
            out_specs=(turned, lse_spec),
            scratch_shapes=[
                pltpu.VMEM((2, 1, span_len), F32),
                pltpu.VMEM((2, 1, span_len), F32),
                pltpu.VMEM((2, HEAD, span_len), F32),
            ],
        ),
        input_output_aliases={len(inputs) + i: i for i in range(len(earlier))},
        cost_estimate=pl.CostEstimate(
            flops=40 * span_len * sum(lengths) * number * LANES, bytes_accessed=span_len * width, transcendentals=0
        ),
        compiler_params=pltpu.CompilerParams(vmem_limit_bytes=ATTEND_BYTES),
        name="attend_forward",
    )(*inputs, *earlier)


def attend_backward(base, final, key_len, queries, queries_t, grad, grad_t, attended_t, lse, low_row, bounds, k, v, acc):
    span_len, width = queries.shape
    pairs = pl.cdiv(width, LANES)
    plain = pl.BlockSpec((span_len, LANES), lambda p, b: (0, p))
    turned = pl.BlockSpec((LANES, span_len), lambda p, b: (p, 0))
    low_spec = pl.BlockSpec((1, span_len), lambda p, b: (0, 0))
    key_spec = pl.BlockSpec((k.shape[0], LANES), lambda p, b: (0, p))
    lse_spec = pl.BlockSpec((1, 2, span_len), lambda p, b: (p, 0, 0))
    acc_spec = pl.BlockSpec((1, 2, HEAD, span_len), lambda p, b: (p, 0, 0, 0))
    sums_spec = pl.BlockSpec((2, LANES), lambda p, b: (0, p))
    inputs = (bounds, queries, queries_t, grad, grad_t, attended_t, lse, low_row, k, v)
    specs = [plain, turned, plain, turned, turned, lse_spec, low_spec, key_spec, key_spec]
    if acc is not None:
        inputs += (acc,)
        specs.append(acc_spec)
    sums = jax.ShapeDtypeStruct((span_len, width), BF16) if final else jax.ShapeDtypeStruct((pairs, 2, HEAD, span_len), F32)
    return pl.pallas_call(
        partial(backward_kernel, base, final, pairs, width - (pairs - 1) * LANES, key_len - span_len),
        out_shape=(
            sums,
            jax.ShapeDtypeStruct(k.shape, BF16),
            jax.ShapeDtypeStruct(k.shape, BF16),
            jax.ShapeDtypeStruct((2, width), F32),
        ),
        grid_spec=pltpu.PrefetchScalarGridSpec(
            num_scalar_prefetch=1,
            grid=(pairs,),
            in_specs=specs,
            out_specs=(plain if final else acc_spec, key_spec, key_spec, sums_spec),
            scratch_shapes=[pltpu.VMEM((2, HEAD, span_len), F32)],
        ),
        cost_estimate=pl.CostEstimate(
            flops=40 * span_len * k.shape[0] * width, bytes_accessed=span_len * width, transcendentals=0
        ),
        compiler_params=pltpu.CompilerParams(vmem_limit_bytes=ATTEND_BYTES),
        name="attend_backward",
    )(*inputs)


def along_group(x, step, count, wrap):
    pairs = [(i, (i + step) % count) for i in range(count) if wrap or 0 <= i + step < count]
    return lax.ppermute(x, "group", pairs)


def hop(rows, step, count):
    bands = rows.reshape(-1, 64, rows.shape[1])
    return along_group(bands, step, count, False).reshape(rows.shape)


def flip(x, bit, count):
    return lax.ppermute(x, "dp", [(i, i ^ bit) for i in range(count)])


CORE, ACROSS, DOWN = 1, 2, 4


def pick(x, index, axis=0):
    return lax.dynamic_index_in_dim(x, index, axis, keepdims=False)


def put(x, part, index):
    start = tuple(index) + (0,) * (x.ndim - len(index))
    part = part.reshape((1,) * len(index) + part.shape)
    return lax.dynamic_update_slice(x, part, start)


def matmul_t(left, right):
    return lax.dot_general(left, right, (((1,), (1,)), ((), ())), preferred_element_type=F32)


def split_rows(core, total_ref, keep_ref, send_ref):
    rows = keep_ref.shape[2]

    def give(first, second):
        for i in range(keep_ref.shape[1]):
            first[0, i] = total_ref[2 * i * rows : (2 * i + 1) * rows, :].astype(BF16)
            second[0, i] = total_ref[(2 * i + 1) * rows : (2 * i + 2) * rows, :].astype(BF16)

    pl.when(core == 0)(lambda: give(keep_ref, send_ref))
    pl.when(core != 0)(lambda: give(send_ref, keep_ref))


def outer_into(left_t, right, total_ref):
    band = total_ref.shape[0] // 4
    for i in range(4):
        total_ref[i * band : (i + 1) * band, :] = jnp.dot(
            left_t[i * band : (i + 1) * band, :], right, preferred_element_type=F32
        )


def feed_kernel(core_ref, x_ref, w_ref, b_ref, g_ref, hidden_ref, slope_ref, keep_ref, send_ref, xt_ref, total_ref):
    @pl.when(pl.program_id(0) == 0)
    def _():
        xt_ref[...] = x_ref[...].T

    span_len = x_ref.shape[0]
    band = span_len // 4
    for i in range(4):
        rows = slice(i * band, (i + 1) * band)
        u = jnp.dot(x_ref[rows, :], w_ref[0], preferred_element_type=F32) + b_ref[0]
        inner = 0.7978845608028654 * (u + 0.044715 * (u * u * u))
        t = jnp.tanh(inner)
        hidden_ref[0, rows, :] = (0.5 * u * (1.0 + t)).astype(BF16)
        slope = 0.5 * (1.0 + t) + 0.5 * u * (1.0 - t * t) * (0.7978845608028654 * (1.0 + 0.134145 * (u * u)))
        slope_ref[0, rows, :] = slope.astype(BF16)
    outer_into(hidden_ref[0].T, g_ref[...], total_ref)
    split_rows(core_ref[0], total_ref, keep_ref, send_ref)


def feed_back_kernel(core_ref, g_ref, wp_ref, slope_ref, xt_ref, wf_ref, keep_ref, send_ref, xg_ref, bg_ref, total_ref):
    grad = matmul_t(g_ref[...], wp_ref[0]) * slope_ref[0].astype(F32)
    low = grad.astype(BF16)
    bg_ref[0] = jnp.sum(low.astype(F32), axis=0, keepdims=True)
    outer_into(xt_ref[...], low, total_ref)
    split_rows(core_ref[0], total_ref, keep_ref, send_ref)
    part = matmul_t(low, wf_ref[0])

    @pl.when(pl.program_id(0) == 0)
    def _():
        xg_ref[...] = part

    @pl.when(pl.program_id(0) != 0)
    def _():
        xg_ref[...] += part


def project_kernel(h_ref, w_ref, r_ref, b_ref, o_ref, total_ref):
    part = jnp.dot(h_ref[0], w_ref[0], preferred_element_type=F32)
    step = pl.program_id(0)

    @pl.when(step == 0)
    def _():
        total_ref[...] = part + (r_ref[...] + b_ref[...])

    @pl.when(step != 0)
    def _():
        total_ref[...] += part

    @pl.when(step == pl.num_programs(0) - 1)
    def _():
        o_ref[...] = total_ref[...].T


def chunk_spec(*shape):
    return pl.BlockSpec((1,) + shape, lambda j, *s: (j,) + (0,) * len(shape))


def whole_spec(*shape):
    return pl.BlockSpec(shape, lambda j, *s: (0,) * len(shape))


def feed_call(kernel, name, scalars, inputs, in_specs, outs, out_specs, scratch, chunks):
    return pl.pallas_call(
        kernel,
        out_shape=outs,
        grid_spec=pltpu.PrefetchScalarGridSpec(
            num_scalar_prefetch=len(scalars),
            grid=(chunks,),
            in_specs=in_specs,
            out_specs=out_specs,
            scratch_shapes=scratch,
        ),
        cost_estimate=pl.CostEstimate(flops=20 * inputs[0].size * inputs[1].shape[-1], bytes_accessed=1024, transcendentals=0),
        compiler_params=pltpu.CompilerParams(vmem_limit_bytes=56 * 1024 * 1024),
        name=name,
    )(*scalars, *inputs)


def feed(core, x, full_fc, bias, grad):
    span_len, width = x.shape
    chunks = full_fc.shape[0]
    rows = width // 8
    part = jax.ShapeDtypeStruct((chunks, 4, rows, width), BF16)
    tall = jax.ShapeDtypeStruct((chunks, span_len, width), BF16)
    return feed_call(
        feed_kernel,
        "feed",
        (core,),
        (x, full_fc, bias, grad),
        [whole_spec(span_len, width), chunk_spec(width, width), chunk_spec(1, width), whole_spec(span_len, width)],
        (tall, tall, part, part, jax.ShapeDtypeStruct((width, span_len), BF16)),
        (
            chunk_spec(span_len, width),
            chunk_spec(span_len, width),
            chunk_spec(4, rows, width),
            chunk_spec(4, rows, width),
            whole_spec(width, span_len),
        ),
        [pltpu.VMEM((width, width), F32)],
        chunks,
    )


def feed_back(core, grad, full_proj, slope, x_t, full_fc):
    span_len, width = grad.shape
    chunks = full_fc.shape[0]
    rows = width // 8
    part = jax.ShapeDtypeStruct((chunks, 4, rows, width), BF16)
    return feed_call(
        feed_back_kernel,
        "feed_back",
        (core,),
        (grad, full_proj, slope, x_t, full_fc),
        [
            whole_spec(span_len, width),
            chunk_spec(width, width),
            chunk_spec(span_len, width),
            whole_spec(width, span_len),
            chunk_spec(width, width),
        ],
        (part, part, jax.ShapeDtypeStruct((span_len, width), F32), jax.ShapeDtypeStruct((chunks, 1, width), F32)),
        (chunk_spec(4, rows, width), chunk_spec(4, rows, width), whole_spec(span_len, width), chunk_spec(1, width)),
        [pltpu.VMEM((width, width), F32)],
        chunks,
    )


def project(hidden, full_proj, resid, bias):
    chunks, span_len, width = hidden.shape
    return feed_call(
        project_kernel,
        "project",
        (),
        (hidden, full_proj, resid, bias),
        [chunk_spec(span_len, width), chunk_spec(width, width), whole_spec(span_len, width), whole_spec(1, width)],
        jax.ShapeDtypeStruct((width, span_len), F32),
        whole_spec(width, span_len),
        [pltpu.VMEM((span_len, width), F32)],
        chunks,
    )


def after(x, *before):
    return lax.optimization_barrier((x,) + before)[0]


def plane_share_near(mine, count):
    return flip(mine, ACROSS, count), flip(mine, DOWN, count)


def plane_share_far(from_x, from_y, count):
    cut = cut_of(from_x)
    return flip(from_x[:, :, :cut], DOWN, count), flip(from_y[:, :, cut:], ACROSS, count)


def cut_of(part):
    return part.shape[2] // 2 // LANES * LANES


def assemble_kernel(groups, kind, here_ref, own_ref, *refs):
    sources, outs, sems = refs[:10], refs[10:-1], refs[-1]
    chip, core, z = here_ref[0], here_ref[1], here_ref[2]
    cut = sources[3].shape[2]

    def place(index, plane, half):
        if kind == "plane":
            return outs[0].at[plane, index, half]
        if kind == "chip":
            return outs[0].at[index, plane, half]
        return outs[index].at[plane, half]

    def move(index, k, wait):
        n = 1 + k * 2 * (groups - 1)
        for side in range(2):
            half = core if side == 0 else 1 - core
            for step in range(groups - 1):
                target = place(index, lax.rem(z - step - 1 + groups, groups), half)
                if k < 3:
                    pairs = [(sources[side * 5 + k].at[step], target)]
                else:
                    pairs = [
                        (sources[side * 5 + 3].at[step], target.at[:, :cut]),
                        (sources[side * 5 + 4].at[step], target.at[:, cut:]),
                    ]
                for src, dst in pairs:
                    copy = pltpu.make_async_copy(src, dst, sems.at[n])
                    copy.wait() if wait else copy.start()
                    n += 1

    if kind == "plane":
        owns = [(own_ref, outs[0].at[z])]
    elif kind == "chip":
        owns = [(own_ref, outs[0].at[:, z])]
    else:
        owns = [(own_ref.at[m], outs[m].at[z]) for m in range(4)]
    last = sems.shape[0] - len(owns)
    owns = [pltpu.make_async_copy(src, dst, sems.at[last + i]) for i, (src, dst) in enumerate(owns)]
    for copy in owns:
        copy.start()
    for wait in (False, True):
        for k in range(4):
            if kind == "apart":
                for m in range(4):
                    pl.when(chip == m ^ k)(partial(move, m, k, wait))
            else:
                move(chip ^ k, k, wait)
    for copy in owns:
        copy.wait()


def assemble(own, sources, here, groups, kind):
    rows, cols = own.shape[2:]
    if kind == "apart":
        shapes = [(groups, 2, rows, cols)] * 4
    else:
        shapes = [(groups, 4, 2, rows, cols) if kind == "plane" else (4, groups, 2, rows, cols)]
    return pl.pallas_call(
        partial(assemble_kernel, groups, kind),
        out_shape=[jax.ShapeDtypeStruct(shape, own.dtype) for shape in shapes],
        grid_spec=pltpu.PrefetchScalarGridSpec(
            num_scalar_prefetch=1,
            grid=(1,),
            in_specs=[pl.BlockSpec(memory_space=pl.ANY)] * 11,
            out_specs=[pl.BlockSpec(shape, lambda i, h, n=len(shape): (0,) * n) for shape in shapes],
            scratch_shapes=[pltpu.SemaphoreType.DMA((1 + 10 * (groups - 1) + 4,))],
        ),
        compiler_params=pltpu.CompilerParams(vmem_limit_bytes=VMEM_BYTES),
        cost_estimate=pl.CostEstimate(flops=0, bytes_accessed=own.size, transcendentals=0),
        name="assemble",
    )(jnp.stack(here).astype(jnp.int32), own, *sources)


def from_planes(piece, groups):
    return jnp.stack([along_group(piece, step, groups, True) for step in range(1, groups)])


def chip_sum(keep, send, count, *during):
    got = flip(send, CORE, count)
    got = after(got, *during) if during else got
    return (keep.astype(F32) + got.astype(F32)).astype(BF16)


def joined(core, keep, send):
    first, second = jnp.where(core == 0, keep, send), jnp.where(core == 0, send, keep)
    both = jnp.stack([first, second], axis=2)
    return both.reshape(both.shape[0], -1, both.shape[-1])


def plane_first_step(half, chip, count, axis):
    to_diag = pick(half, chip ^ 3, axis)
    cut = to_diag.shape[0] // 2
    return flip(to_diag[:cut], ACROSS, count), flip(to_diag[cut:], DOWN, count)


def plane_second_step(half, via, chip, count, axis):
    to_own, to_x, to_y = (pick(half, chip ^ k, axis) for k in range(3))
    cut = to_own.shape[0] // 2
    from_y = flip(jnp.concatenate([to_y[:cut] + via[0], to_y[cut:]]), DOWN, count)
    from_x = flip(jnp.concatenate([to_x[:cut], to_x[cut:] + via[1]]), ACROSS, count)
    return to_own, from_x, from_y


def second_sum(to_own, from_x, from_y):
    return (to_own.astype(F32) + from_x.astype(F32) + from_y.astype(F32)).astype(BF16)


def line_parts(mine, z, groups):
    sent = [(pick(mine, lax.rem(z + step, groups)), step) for step in range(1, groups)]
    return [pick(mine, z)] + [along_group(part, step, groups, True) for part, step in sent]


def parts_sum(parts):
    total = parts[0].astype(F32)
    for part in parts[1:]:
        total = total + part.astype(F32)
    return total


def line_sum(mine, z, groups):
    return parts_sum(line_parts(mine, z, groups))


def shares_of(mine, near, far):
    return jnp.concatenate((mine,) + near + (jnp.concatenate(far, axis=2),))


def in_vmem():
    return pl.BlockSpec(memory_space=pltpu.VMEM)


def norm_back_kernel(parts, turned, values_ref, gain_ref, base_ref, *refs):
    grads, (out_ref, low_ref, gain_sum_ref, shift_sum_ref, low_sum_ref) = refs[:parts], refs[parts:]
    values = values_ref[...].astype(F32)
    grad = grads[0][...].astype(F32)
    for other in grads[1:]:
        grad = grad + other[...].astype(F32)
    center = values - jnp.mean(values, axis=-1, keepdims=True)
    scale = lax.rsqrt(jnp.mean(center * center, axis=-1, keepdims=True) + EPSILON)
    unit = center * scale
    inner = grad * gain_ref[...]
    back = scale * (
        inner - jnp.mean(inner, axis=-1, keepdims=True) - unit * jnp.mean(inner * unit, axis=-1, keepdims=True)
    )
    out = base_ref[...].astype(F32) + back
    out_ref[...] = out.T if turned else out
    low = out.astype(BF16)
    low_ref[...] = low
    sums = (
        jnp.sum(grad * unit, axis=0, keepdims=True),
        jnp.sum(grad, axis=0, keepdims=True),
        jnp.sum(low.astype(F32), axis=0, keepdims=True),
    )
    begun = pl.program_id(0) != 0
    for ref, part in zip((gain_sum_ref, shift_sum_ref, low_sum_ref), sums):
        ref[...] = jnp.where(begun, ref[...], 0.0) + part


def norm_back(values, gain, base, *grads, turned=False):
    span_len, width = values.shape
    band = min(span_len, LANES)
    columns = pl.BlockSpec((width, band), lambda i: (0, i))
    rows = pl.BlockSpec((band, width), lambda i: (i, 0))
    line = pl.BlockSpec((1, width), lambda i: (0, 0))
    sums = jax.ShapeDtypeStruct((1, width), F32)
    out, low, gain_sum, shift_sum, low_sum = pl.pallas_call(
        partial(norm_back_kernel, len(grads), turned),
        out_shape=(
            jax.ShapeDtypeStruct((width, span_len) if turned else (span_len, width), F32),
            jax.ShapeDtypeStruct((span_len, width), BF16),
            sums,
            sums,
            sums,
        ),
        grid=(span_len // band,),
        in_specs=[rows, line, rows] + [rows] * len(grads),
        out_specs=(columns if turned else rows, rows, line, line, line),
        cost_estimate=pl.CostEstimate(flops=0, bytes_accessed=1024, transcendentals=0),
        compiler_params=pltpu.CompilerParams(vmem_limit_bytes=VMEM_BYTES),
        name="norm_back",
    )(values, gain[None], base, *grads)
    return out, low, gain_sum, shift_sum, low_sum


def key_back_kernel(dk_ref, dv_ref, wk_ref, wv_ref, *refs):
    out_ref = refs[-1]
    total = matmul_t(dk_ref[...], wk_ref[...]) + matmul_t(dv_ref[...], wv_ref[...])
    for other in refs[:-1]:
        total = total + other[...].astype(F32)
    out_ref[...] = total.astype(out_ref.dtype)


def key_back(dk, dv, full_k, full_v, moving, kind):
    more = () if moving is None else (moving,)
    return pl.pallas_call(
        key_back_kernel,
        out_shape=jax.ShapeDtypeStruct(dk.shape, kind),
        in_specs=[in_vmem()] * (4 + len(more)),
        out_specs=in_vmem(),
        cost_estimate=pl.CostEstimate(flops=0, bytes_accessed=1024, transcendentals=0),
        compiler_params=pltpu.CompilerParams(vmem_limit_bytes=VMEM_BYTES),
        name="key_back",
    )(dk, dv, full_k, full_v, *more)


def attn_grads_kernel(blocks, core_ref, *refs):
    normed, dks, dvs = refs[:blocks], refs[blocks : 2 * blocks], refs[2 * blocks : 3 * blocks]
    dq_ref, ot_ref, low_ref, keep_ref, send_ref, total_ref, turned_ref = refs[3 * blocks :]
    span_len = dq_ref.shape[0]
    step = pl.program_id(0)
    width = total_ref.shape[0]
    band = width // 4

    def sums(rights):
        for i in range(4):
            rows = slice(i * band, (i + 1) * band)
            total = None
            for b, right in enumerate(rights):
                if right is None:
                    continue
                part = jnp.dot(turned_ref[b, rows, :], right, preferred_element_type=F32)
                total = part if total is None else total + part
            total_ref[rows, :] = total

    @pl.when(step == 0)
    def _():
        begin = 0
        for ref in normed:
            for at in range(0, ref.shape[0], span_len):
                turned_ref[begin // span_len] = ref[at : at + span_len, :].T
                begin += span_len
        sums([None] * (turned_ref.shape[0] - 1) + [dq_ref[...]])

    def pieces(group):
        return [ref[at : at + span_len, :] for ref in group for at in range(0, ref.shape[0], span_len)]

    pl.when(step == 1)(lambda: sums(pieces(dks)))
    pl.when(step == 2)(lambda: sums(pieces(dvs)))

    @pl.when(step == 3)
    def _():
        outer_into(ot_ref[...], low_ref[...], total_ref)

    split_rows(core_ref[0], total_ref, keep_ref, send_ref)


def attn_grads(core, normed, dks, dvs, dq, attended_t, low):
    span_len, width = dq.shape
    rows = width // 8
    key_len = sum(block.shape[0] for block in normed)
    part = jax.ShapeDtypeStruct((4, 4, rows, width), BF16)
    inputs = (*normed, *dks, *dvs, dq, attended_t, low)
    return pl.pallas_call(
        partial(attn_grads_kernel, len(normed)),
        out_shape=(part, part),
        grid_spec=pltpu.PrefetchScalarGridSpec(
            num_scalar_prefetch=1,
            grid=(4,),
            in_specs=[in_vmem()] * len(inputs),
            out_specs=(chunk_spec(4, rows, width), chunk_spec(4, rows, width)),
            scratch_shapes=[
                pltpu.VMEM((width, width), F32),
                pltpu.VMEM((key_len // span_len, width, span_len), BF16),
            ],
        ),
        cost_estimate=pl.CostEstimate(flops=20 * span_len * width * width, bytes_accessed=1024, transcendentals=0),
        compiler_params=pltpu.CompilerParams(vmem_limit_bytes=56 * 1024 * 1024),
        name="attn_grads",
    )(core, *inputs)


def give_out_kernel(kind, here_ref, mine_ref, other_ref, *outs):
    chip, core = here_ref[0], here_ref[1]
    rows, cols = mine_ref.shape[1:]
    for side, ref in enumerate((mine_ref, other_ref)):
        half = core if side == 0 else 1 - core
        for k in range(4):
            piece = ref[k].astype(F32)
            if kind == "plane":
                at = pl.ds(pl.multiple_of(((chip ^ k) * 2 + half) * rows, 8), rows)
                outs[0][at, :] = piece
                continue
            at = pl.ds(pl.multiple_of(half * rows, 8), rows)
            for m in range(4):

                @pl.when(chip == m ^ k)
                def _(m=m, at=at, piece=piece):
                    if kind == "apart":
                        outs[m][at, :] = piece
                    else:
                        outs[0][at, m * cols : (m + 1) * cols] = piece


def give_out(shares, other, here, kind):
    rows, cols = shares.shape[1:]
    shapes = {"apart": [(2 * rows, cols)] * 4, "chip": [(2 * rows, 4 * cols)], "plane": [(8 * rows, cols)]}[kind]
    return pl.pallas_call(
        partial(give_out_kernel, kind),
        out_shape=[jax.ShapeDtypeStruct(shape, F32) for shape in shapes],
        grid_spec=pltpu.PrefetchScalarGridSpec(
            num_scalar_prefetch=1,
            grid=(1,),
            in_specs=[whole_spec(4, rows, cols)] * 2,
            out_specs=[whole_spec(*shape) for shape in shapes],
        ),
        cost_estimate=pl.CostEstimate(flops=0, bytes_accessed=1024, transcendentals=0),
        compiler_params=pltpu.CompilerParams(vmem_limit_bytes=VMEM_BYTES),
        name="give_out",
    )(jnp.stack(here).astype(jnp.int32), shares, other)


def mean_spread(values):
    center = values - jnp.mean(values, axis=-1, keepdims=True)
    spread = jnp.mean(center * center, axis=-1, keepdims=True)
    return center, lax.rsqrt(spread + EPSILON)


def layer_norm(values, gain, shift):
    center, scale = mean_spread(values)
    return center * scale * gain + shift


def layer_norm_back(values, gain, grad):
    center, scale = mean_spread(values)
    unit = center * scale
    inner = grad * gain
    back = scale * (
        inner
        - jnp.mean(inner, axis=-1, keepdims=True)
        - unit * jnp.mean(inner * unit, axis=-1, keepdims=True)
    )
    return back, jnp.sum(grad * unit, axis=0), jnp.sum(grad, axis=0)


def row_sum(values):
    return jnp.sum(values.astype(F32), axis=0)


def matmul(left, right):
    return jnp.dot(left, right, preferred_element_type=F32)


def weight_grad(left, right):
    return jnp.einsum("ra,rb->ab", left, right, preferred_element_type=F32).astype(BF16)


def back_through(grad_rows, weight):
    return jnp.einsum("rb,ab->ra", grad_rows, weight, preferred_element_type=F32)


def on_device(
    count,
    groups,
    tokens,
    segments,
    out_grad,
    norm1_gain,
    norm1_bias,
    w_query,
    query_bias,
    w_key,
    w_value,
    value_bias,
    w_out,
    out_bias,
    norm2_gain,
    norm2_bias,
    w_fc,
    fc_bias,
    w_proj,
    proj_bias,
):
    _, span_len, width = tokens.shape
    shard = width // groups
    half = shard // 2
    chunks = w_fc.shape[1] // width
    key_len = segments.shape[1]
    z = lax.axis_index("group")
    place = lax.axis_index("dp")
    fast = count == 8 and groups == 4 and chunks == 4
    chip, core = place // 2, lax.rem(place, 2)
    here = (chip, core, z)
    forward_parts = attend_parts(pl.cdiv(width, LANES), 3)

    small = jnp.concatenate(
        [norm1_gain, norm1_bias, query_bias, value_bias, out_bias, norm2_gain, norm2_bias, proj_bias, fc_bias]
    )
    small_rel = jnp.stack([small] + [along_group(small, step, groups, True) for step in range(1, groups)])
    small_all = jnp.take(small_rel, lax.rem(z - jnp.arange(groups) + groups, groups), axis=0)
    vectors = small_all[:, : 8 * shard].reshape(groups, 8, shard).transpose(1, 0, 2).reshape(8, width)
    gain_one, shift_one, bias_q, bias_v, bias_o, gain_two, shift_two, bias_p = vectors.astype(F32)
    bias_fc = small_all[:, 8 * shard :].astype(F32).reshape(chunks, 1, width)

    mine = tokens[0]
    inputs = mine.astype(F32)
    normed_one = layer_norm(inputs, gain_one, shift_one).astype(BF16)
    own_base = key_len - span_len
    if fast:
        attn_own = jnp.stack([w_query, w_key, w_value, w_out]).reshape(4, 2, half, width)
        attn_ring = from_planes(pick(pick(attn_own, chip), core), groups)
        attn_near = plane_share_near(attn_ring, count)
        hops = [mine, hop(after(mine, attn_ring, small_rel), 1, groups)]
        attn_three = (attn_ring,) + attn_near
        attn_far = plane_share_far(*attn_near, count)
        attn_other = tuple(flip(after(part, *attn_near), CORE, count) for part in attn_three)
        attn_other += tuple(flip(after(part, hops[1]), CORE, count) for part in attn_far)
        hops.append(hop(hops[1], 1, groups))
        attn = assemble(attn_own, attn_three + attn_far + attn_other, here, groups, "apart")
        full_q, full_k, full_v, full_o = (part.reshape(width, width) for part in attn)
        normed_one, hops[2] = lax.optimization_barrier((normed_one, hops[2]))
        hops.append(hop(hops[2], 1, groups))
    else:
        gather = partial(lax.all_gather, axis_name="group", axis=0, tiled=True)
        full_q, full_k, full_v, full_o = (gather(w) for w in (w_query, w_key, w_value, w_out))
        full_fc = gather(w_fc).reshape(width, chunks, width).transpose(1, 0, 2)
        full_proj = gather(w_proj).reshape(chunks, width, width)
    queries_t = (jnp.einsum("td,df->ft", normed_one, full_q, preferred_element_type=F32) + bias_q[:, None]).astype(BF16)
    queries = (matmul(normed_one, full_q) + bias_q).astype(BF16)

    def keys_of(normed):
        return matmul(normed, full_k).astype(BF16), (matmul(normed, full_v) + bias_v).astype(BF16)

    def norm_of(block):
        return layer_norm(block.astype(F32), gain_one, shift_one).astype(BF16)

    if fast:
        own_keys = keys_of(normed_one)
        fc_own = w_fc.reshape(2, half, chunks, width).transpose(2, 0, 1, 3)
        fc_piece = pick(pick(fc_own, chip), core)
        proj_own = w_proj.reshape(4, 2, half, width)
        proj_piece = pick(pick(proj_own, chip), core)
        normed = [normed_one, norm_of(hops[1]), norm_of(hops[2])]
        both = [own_keys] + [keys_of(block) for block in normed[1:]]
        hops[3] = after(hops[3], *both[1], *both[2])
        fc_ring = from_planes(after(fc_piece, hops[3]), groups)
        normed.append(norm_of(hops[3]))
        both.append(keys_of(normed[3]))
        normed, keys, values = normed[::-1], [b[0] for b in both[::-1]], [b[1] for b in both[::-1]]
    else:
        hops = [mine]
        for _ in range(groups - 1):
            hops.append(hop(hops[-1], 1, groups))
        normed = [norm_of(jnp.concatenate(hops[::-1]))]
        both = keys_of(normed[0])
        keys, values = [both[0]], [both[1]]

    seg = segments[0]
    seg_mine = lax.dynamic_slice_in_dim(seg, z * span_len, span_len)
    low_row = jnp.sum((seg[None, :] < seg_mine[:, None]).astype(jnp.int32), axis=1)
    low_row = low_row + (groups - 1 - z) * span_len
    tile_len = tile_length(span_len)
    low_tile = low_row[0] // tile_len
    mid_tile = jnp.clip((low_row[-1] + tile_len - 1) // tile_len, low_tile, own_base // tile_len)
    bounds = jnp.stack([low_tile, mid_tile]).astype(jnp.int32)
    low_row = low_row[None]

    state = None
    for number, part in enumerate(forward_parts):
        row_now = after(low_row, queries) if number == 0 else low_row
        if fast and number == 1:
            fc_near = plane_share_near(after(fc_ring, state[0]), count)
            proj_ring = from_planes(after(proj_piece, fc_ring, state[0]), groups)
            row_now = after(low_row, fc_ring)
        if fast and number == 2:
            fc_three = (fc_ring,) + fc_near
            fc_far = plane_share_far(*(after(part, state[0]) for part in fc_near), count)
            fc_other = tuple(flip(after(part, state[0], *fc_near), CORE, count) for part in fc_three)
            proj_near = plane_share_near(after(proj_ring, state[0], *fc_near), count)
            row_now = after(low_row, proj_ring, *fc_near)
        state = attend_forward(part, queries_t, keys, values, row_now, bounds, state)
    attended_t, lse = state
    if fast:
        fc_other += tuple(flip(after(part, attended_t), CORE, count) for part in fc_far)
        attended_t = after(attended_t, *fc_far)
    resid = inputs + jnp.einsum("ft,fd->td", attended_t, full_o, preferred_element_type=F32) + bias_o
    normed_two = layer_norm(resid, gain_two, shift_two).astype(BF16)
    if fast:
        full_fc = assemble(after(fc_own, normed_two), fc_three + fc_far + fc_other, here, groups, "chip")
        full_fc = full_fc[0].reshape(4, width, width)

    cot = out_grad[0]
    proj_bias_grad = row_sum(cot)
    which = jnp.reshape(core, (1,)).astype(jnp.int32)
    if fast:
        normed_two = after(normed_two, *proj_near)
    hidden, slope, proj_keep, proj_send, normed_two_t = feed(which, normed_two, full_fc, bias_fc, cot)
    cot_now = cot
    if fast:
        proj_three = (proj_ring,) + proj_near
        proj_far = plane_share_far(*(after(part, normed_two) for part in proj_near), count)
        proj_other = tuple(flip(after(part, normed_two, *proj_near), CORE, count) for part in proj_three)
        proj_send, *proj_moved = lax.optimization_barrier((proj_send, *proj_far, *proj_other))
        proj_far, proj_other = tuple(proj_moved[:2]), tuple(proj_moved[2:])
        proj_other += tuple(flip(part, CORE, count) for part in proj_far)
        full_proj = assemble(proj_own, proj_three + proj_far + proj_other, here, groups, "plane")
        full_proj = full_proj[0].reshape(4, width, width)
        proj_chip = chip_sum(proj_keep, proj_send, count)
        cot_now, proj_chip = lax.optimization_barrier((cot, proj_chip))
        proj_via = plane_first_step(proj_chip, chip, count, 1)
    fc_keep, fc_send, normed_two_grad, fc_bias_grad = feed_back(which, cot_now, full_proj, slope, normed_two_t, full_fc)
    if fast:
        normed_two_grad = after(normed_two_grad, *proj_via)
    resid_grad, resid_low, gain_two_grad, shift_two_grad, out_bias_grad = norm_back(
        resid, gain_two, cot, normed_two_grad
    )
    attended_grad = back_through(resid_low, full_o).astype(BF16)
    attended_grad_t = jnp.einsum("td,fd->ft", resid_low, full_o, preferred_element_type=F32).astype(BF16)
    if fast:
        proj_mine = plane_second_step(proj_chip, proj_via, chip, count, 1)
        fc_chip = chip_sum(fc_keep, after(fc_send, *proj_via), count, attended_grad)
        fc_via = plane_first_step(fc_chip, chip, count, 0)
    acc, moving, base = None, None, 0
    dks, dvs, value_bias_grad = [], [], 0.0
    for number, (k, v) in enumerate(zip(keys, values)):
        row_now = low_row
        final = number == len(keys) - 1
        if fast and number == 0:
            row_now = after(low_row, fc_chip)
        if fast and number == 1:
            row_now = after(low_row, sent, proj_mine)
        if fast and number == 2:
            row_now = after(low_row, sent, proj_line)
        if fast and number == 3:
            row_now = after(low_row, sent, fc_mine, *proj_line_near)
        acc, dk, dv, sums = attend_backward(
            base, final, key_len, queries, queries_t, attended_grad, attended_grad_t, attended_t, lse, row_now, bounds, k, v, acc
        )
        base += k.shape[0]
        dks.append(dk)
        dvs.append(dv)
        value_bias_grad = value_bias_grad + sums[:1]
        if final:
            break
        if number > 0:
            moving = after(moving, acc)
        sent = key_back(dk, dv, full_k, full_v, moving, BF16)
        if number == 0:
            sent = after(sent, *fc_via)
        moving = hop(sent, -1, groups)
        if number == 0:
            proj_mine = second_sum(*(after(part, sent) for part in proj_mine))
            proj_lines = line_parts(proj_mine, z, groups)
        if number == 1:
            proj_line = parts_sum([after(part, sent) for part in proj_lines]).astype(BF16)
            proj_line_near = plane_share_near(proj_line[None], count)
            fc_mine = plane_second_step(fc_chip, fc_via, chip, count, 0)
        if number == 2:
            fc_mine = second_sum(*(after(part, sent) for part in fc_mine))
            proj_line_near = tuple(after(part, sent) for part in proj_line_near)
            proj_line_far = plane_share_far(*proj_line_near, count)
    dqueries, query_bias_grad = acc, sums[1:]
    dqueries_now = dqueries
    if fast:
        norm_term = key_back(dk, dv, full_k, full_v, after(moving, acc), F32)
        fc_lines = line_parts(after(fc_mine, norm_term), z, groups)
        proj_line_far = tuple(after(part, norm_term) for part in proj_line_far)
        proj_shares = shares_of(proj_line[None], proj_line_near, proj_line_far)
        proj_others = flip(proj_shares, CORE, count)
        dqueries_now = after(dqueries, norm_term, *proj_line_far)
    else:
        norm_term = back_through(dk, full_k) + back_through(dv, full_v)
        for step in range(groups - 1):
            part = norm_term[step * span_len : (step + 1) * span_len]
            moving = hop((part if moving is None else part + moving.astype(F32)).astype(BF16), -1, groups)
        norm_term = norm_term[own_base:] + moving.astype(F32)
    attn_keep, attn_send = attn_grads(which, normed, dks, dvs, dqueries_now, attended_t, resid_low)
    dqueries_now = dqueries
    if fast:
        fc_line = parts_sum([after(part, attn_send) for part in fc_lines]).astype(BF16)
        attn_chip = chip_sum(attn_keep, after(attn_send, fc_line), count)
        fc_line_near = plane_share_near(fc_line[None], count)
        attn_via = plane_first_step(attn_chip, chip, count, 0)
        fc_line_near = tuple(after(part, attn_chip) for part in fc_line_near)
        fc_line_far = plane_share_far(*fc_line_near, count)
        attn_mine = plane_second_step(attn_chip, attn_via, chip, count, 0)
        fc_line_far = tuple(after(part, *attn_via) for part in fc_line_far)
        fc_shares = shares_of(fc_line[None], fc_line_near, fc_line_far)
        fc_others = flip(fc_shares, CORE, count)
        dqueries_now = after(dqueries, *attn_via)
        (proj_sum,) = give_out(after(proj_shares, *attn_via), proj_others, here, "plane")
    normed_one_grad = back_through(dqueries_now, full_q)
    tokens_grad, _, gain_one_grad, shift_one_grad, _ = norm_back(
        mine, gain_one, resid_grad, normed_one_grad, norm_term, turned=True
    )
    vector_sums = jnp.concatenate(
        [
            gain_one_grad,
            shift_one_grad,
            query_bias_grad,
            value_bias_grad,
            out_bias_grad,
            gain_two_grad,
            shift_two_grad,
            proj_bias_grad[None],
            fc_bias_grad.reshape(chunks, width),
        ]
    )
    vector_sums = parts_sum([vector_sums] + [along_group(vector_sums, step, groups, True) for step in range(1, groups)])
    hidden_now = hidden
    if fast:
        (fc_sum,) = give_out(after(fc_shares, proj_sum), fc_others, here, "chip")
        attn_mine = second_sum(*(after(part, proj_sum, fc_sum, tokens_grad) for part in attn_mine))
        attn_line = line_parts(attn_mine, z, groups)
        vector_sums = vector_sums + flip(vector_sums, CORE, count)
        hidden_now = after(hidden, attn_mine, vector_sums)
    activations = project(hidden_now, full_proj, resid, bias_p[None])
    if fast:
        vector_sums = vector_sums + after(flip(vector_sums, ACROSS, count), activations)
        attn_line = [after(part, vector_sums) for part in attn_line]
        vector_sums = vector_sums + flip(vector_sums, DOWN, count)
    else:
        bit = 1
        while bit < count:
            vector_sums = vector_sums + flip(vector_sums, bit, count)
            bit *= 2
    if fast:
        attn_line = parts_sum([after(part, activations) for part in attn_line]).astype(BF16)
        attn_near = plane_share_near(attn_line[None], count)
        attn_far = plane_share_far(*attn_near, count)
        attn_shares = shares_of(attn_line[None], attn_near, attn_far)
        attn_others = flip(attn_shares, CORE, count)
        q_sum, k_sum, v_sum, out_sum = give_out(attn_shares, attn_others, here, "apart")

    eight = lax.dynamic_slice_in_dim(vector_sums[:8], z * shard, shard, 1)
    fc_bias_sum = lax.dynamic_slice_in_dim(vector_sums[8:].reshape(-1), z * fc_bias.shape[0], fc_bias.shape[0])
    if not fast:

        def whole_sum(part):
            part = lax.psum_scatter(part, "group", scatter_dimension=0, tiled=True)
            return lax.psum(part.astype(F32), "dp")

        proj_sum = whole_sum(joined(core, proj_keep, proj_send).reshape(chunks * width, width))
        fc_sum = whole_sum(joined(core, fc_keep, fc_send).transpose(1, 0, 2).reshape(width, chunks * width))
        attn_whole = joined(core, attn_keep, attn_send)
        q_sum, k_sum, v_sum, out_sum = (whole_sum(attn_whole[m]) for m in range(4))
    return (
        activations.T[None],
        tokens_grad.T[None],
        eight[0],
        eight[1],
        q_sum,
        eight[2],
        k_sum,
        v_sum,
        eight[3],
        out_sum,
        eight[4],
        eight[5],
        eight[6],
        fc_sum,
        fc_bias_sum,
        proj_sum,
        eight[7],
    )


def solution(mesh):
    rows, vec, mat = P("dp", "group", None), P("group"), P("group", None)
    weights = (vec, vec, mat, vec, mat, mat, vec, mat, vec, vec, vec, mat, vec, mat, vec)
    return jax.shard_map(
        partial(on_device, mesh.shape["dp"], mesh.shape["group"]),
        mesh=mesh,
        in_specs=(rows, P("dp", None), rows) + weights,
        out_specs=(rows, rows) + weights,
        check_vma=False,
    )
```

```python
from functools import partial

import jax
import jax.numpy as jnp
from jax import lax
from jax.experimental import pallas as pl
from jax.experimental.pallas import tpu as pltpu
from jax.sharding import PartitionSpec as P

HEAD = 64
LANES = 128
EPSILON = 1e-05
NEG_FILL = -1e30
F32 = jnp.float32
BF16 = jnp.bfloat16
SCALE = HEAD ** (-0.5)
VMEM_BYTES = 40 * 1024 * 1024
ATTEND_BYTES = 20 * 1024 * 1024
FULL_BYTES = 52 * 1024 * 1024


def tile_length(length):
    return 512 if length % 512 == 0 else length


def keep_of(tile_base, tile_len, low_row, own_base):
    span_len = low_row.shape[1]
    key_pos = tile_base + lax.broadcasted_iota(jnp.int32, (tile_len, span_len), 0)
    query_pos = own_base + lax.broadcasted_iota(jnp.int32, (tile_len, span_len), 1)
    return (key_pos >= low_row) & (key_pos <= query_pos)


def each_tile(bounds_ref, tile, base, length, own_base, unread=None):
    size = tile_length(length)
    half = size // 2
    least, greatest = bounds_ref[0], bounds_ref[1]
    for first in range(0, length, size):
        begin = base + first
        whole = least < begin + half
        upper = (least >= begin + half) & (least < begin + size)
        if begin + size > own_base:
            pl.when(whole)(partial(tile, first, size, True))
        else:
            pl.when(whole & (greatest > begin))(partial(tile, first, size, True))
            pl.when(whole & (greatest <= begin))(partial(tile, first, size, False))
        pl.when(upper)(partial(tile, first + half, half, True))
        if unread is not None:
            pl.when(upper)(partial(unread, first, half))
            pl.when(least >= begin + size)(partial(unread, first, size))


def inside(x, axis, valid):
    where = lax.broadcasted_iota(jnp.int32, x.shape, axis)
    return jnp.where(where < valid, x, jnp.zeros((), x.dtype))


def halves(x, axis):
    where = lax.broadcasted_iota(jnp.int32, x.shape, axis)
    zero = jnp.zeros((), x.dtype)
    return jnp.where(where < HEAD, x, zero), jnp.where(where >= HEAD, x, zero)


def forward_kernel(first, pairs, last_half, lengths, bounds_ref, qt_ref, low_ref, *refs):
    blocks = len(lengths)
    k_refs, v_refs = refs[:blocks], refs[blocks : 2 * blocks]
    ot_ref, lse_ref, max_ref, sum_ref, acc_ref = refs[-5:]
    span_len = qt_ref.shape[1]
    own_base = sum(lengths) - span_len
    last = pl.program_id(0) + first == pairs - 1
    valid = jnp.where(last, last_half, LANES)
    heads = halves(inside((qt_ref[...].astype(F32) * SCALE).astype(BF16), 0, valid), 0)
    max_ref[...] = jnp.full_like(max_ref, NEG_FILL)
    sum_ref[...] = jnp.zeros_like(sum_ref)
    acc_ref[...] = jnp.zeros_like(acc_ref)
    base = 0
    for k_ref, v_ref, length in zip(k_refs, v_refs, lengths):

        def tile(first_row, tile_len, masked, k_ref=k_ref, v_ref=v_ref, base=base):
            rows = slice(first_row, first_row + tile_len)
            k_tile = inside(k_ref[rows, :], 1, valid)
            v_t = v_ref[rows, :].T
            if masked:
                keep = keep_of(base + first_row, tile_len, low_ref[...], own_base)

            def one(head):
                scores = jnp.dot(k_tile, heads[head], preferred_element_type=F32)
                if masked:
                    scores = jnp.where(keep, scores, NEG_FILL)
                old_max = max_ref[head]
                new_max = jnp.maximum(old_max, jnp.max(scores, axis=0, keepdims=True))
                shrink = jnp.exp(old_max - new_max)
                probs = jnp.exp(scores - new_max)
                max_ref[head] = new_max
                sum_ref[head] = sum_ref[head] * shrink + jnp.sum(probs, axis=0, keepdims=True)
                acc_ref[head] = acc_ref[head] * shrink + jnp.dot(
                    v_t[head * HEAD : (head + 1) * HEAD], probs.astype(BF16), preferred_element_type=F32
                )

            @pl.when(valid > HEAD)
            def _():
                one(0)
                one(1)

            @pl.when(valid <= HEAD)
            def _():
                one(0)

        each_tile(bounds_ref, tile, base, length, own_base)
        base += length
    safe = jnp.where(sum_ref[...] > 0, sum_ref[...], 1.0)
    ot_ref[...] = jnp.concatenate([acc_ref[0] / safe[0], acc_ref[1] / safe[1]], axis=0).astype(BF16)
    lse_ref[0] = jnp.concatenate([max_ref[0] + jnp.log(safe[0]), max_ref[1] + jnp.log(safe[1])], axis=0)


def backward_kernel(
    base, final, pairs, last_half, own_base, bounds_ref, q_ref, qt_ref, g_ref, gt_ref, ot_ref, lse_ref, low_ref, k_ref, v_ref, *refs
):
    first = base == 0
    acc_in = None if first else refs[0]
    acc_out, dk_ref, dv_ref, sums_ref, acc_ref = refs[-5:]
    last = pl.program_id(0) == pairs - 1
    valid = jnp.where(last, last_half, LANES)
    q_heads = halves(inside((q_ref[...].astype(F32) * SCALE).astype(BF16), 1, valid), 1)
    qt_heads = halves(inside((qt_ref[...].astype(F32) * SCALE).astype(BF16), 0, valid), 0)
    g_heads = halves(inside(g_ref[...], 1, valid), 1)
    gt_now = inside(gt_ref[...], 0, valid)
    gt_heads = halves(gt_now, 0)
    prod = gt_now.astype(F32) * inside(ot_ref[...], 0, valid).astype(F32)
    deltas = [jnp.sum(prod[h * HEAD : (h + 1) * HEAD], axis=0, keepdims=True) for h in range(2)]
    if first:
        acc_ref[...] = jnp.zeros_like(acc_ref)
    else:
        acc_ref[...] = acc_in[0]

    def tile(first_row, tile_len, masked):
        rows = slice(first_row, first_row + tile_len)
        k_tile = inside(k_ref[rows, :], 1, valid)
        v_tile = inside(v_ref[rows, :], 1, valid)
        k_t = k_tile.T
        if masked:
            keep = keep_of(base + first_row, tile_len, low_ref[...], own_base)

        def one(head):
            scores = jnp.dot(k_tile, qt_heads[head], preferred_element_type=F32)
            probs = jnp.exp(scores - lse_ref[0, head : head + 1])
            if masked:
                probs = jnp.where(keep, probs, 0.0)
            dprobs = jnp.dot(v_tile, gt_heads[head], preferred_element_type=F32)
            dscores = (probs * (dprobs - deltas[head])).astype(BF16)
            dv = jnp.dot(probs.astype(BF16), g_heads[head], preferred_element_type=F32)
            dk = jnp.dot(dscores, q_heads[head], preferred_element_type=F32)
            acc_ref[head] += jnp.dot(k_t[head * HEAD : (head + 1) * HEAD], dscores, preferred_element_type=F32)
            return dk, dv

        def write(dk, dv):
            dk_ref[rows, :] = dk.astype(BF16)
            dv_ref[rows, :] = dv.astype(BF16)

        @pl.when(valid > HEAD)
        def _():
            dk_a, dv_a = one(0)
            dk_b, dv_b = one(1)
            write(dk_a + dk_b, dv_a + dv_b)

        @pl.when(valid <= HEAD)
        def _():
            write(*one(0))

    def clear(first_row, tile_len):
        rows = slice(first_row, first_row + tile_len)
        dk_ref[rows, :] = jnp.zeros((tile_len, LANES), BF16)
        dv_ref[rows, :] = jnp.zeros((tile_len, LANES), BF16)

    each_tile(bounds_ref, tile, base, k_ref.shape[0], own_base, clear)
    dv_sum = jnp.sum(dv_ref[...].astype(F32), axis=0, keepdims=True)
    if final:
        dq = (jnp.concatenate([acc_ref[0], acc_ref[1]], axis=0).T * SCALE).astype(BF16)
        acc_out[...] = dq
        sums_ref[...] = jnp.concatenate([dv_sum, jnp.sum(dq.astype(F32), axis=0, keepdims=True)], axis=0)
    else:
        acc_out[0] = acc_ref[...]
        sums_ref[...] = jnp.concatenate([dv_sum, jnp.zeros_like(dv_sum)], axis=0)


def attend_parts(pairs, number):
    size = pl.cdiv(pairs, number)
    return [(first, min(size, pairs - first)) for first in range(0, pairs, size)]


def attend_forward(part, queries_t, keys, values, low_row, bounds, earlier):
    first, number = part
    width, span_len = queries_t.shape
    pairs = pl.cdiv(width, LANES)
    lengths = tuple(block.shape[0] for block in keys)
    turned = pl.BlockSpec((LANES, span_len), lambda p, b: (p + first, 0))
    low_spec = pl.BlockSpec((1, span_len), lambda p, b: (0, 0))
    key_specs = [pl.BlockSpec((length, LANES), lambda p, b: (0, p + first)) for length in lengths]
    lse_spec = pl.BlockSpec((1, 2, span_len), lambda p, b: (p + first, 0, 0))
    inputs = (bounds, queries_t, low_row) + tuple(keys) + tuple(values)
    earlier = () if earlier is None else tuple(earlier)
    return pl.pallas_call(
        partial(forward_kernel, first, pairs, width - (pairs - 1) * LANES, lengths),
        out_shape=(
            jax.ShapeDtypeStruct((width, span_len), BF16),
            jax.ShapeDtypeStruct((pairs, 2, span_len), F32),
        ),
        grid_spec=pltpu.PrefetchScalarGridSpec(
            num_scalar_prefetch=1,
            grid=(number,),
            in_specs=[turned, low_spec] + key_specs + key_specs + [pl.BlockSpec(memory_space=pl.ANY)] * len(earlier),
            out_specs=(turned, lse_spec),
            scratch_shapes=[
                pltpu.VMEM((2, 1, span_len), F32),
                pltpu.VMEM((2, 1, span_len), F32),
                pltpu.VMEM((2, HEAD, span_len), F32),
            ],
        ),
        input_output_aliases={len(inputs) + i: i for i in range(len(earlier))},
        cost_estimate=pl.CostEstimate(
            flops=40 * span_len * sum(lengths) * number * LANES, bytes_accessed=span_len * width, transcendentals=0
        ),
        compiler_params=pltpu.CompilerParams(vmem_limit_bytes=ATTEND_BYTES),
        name="attend_forward",
    )(*inputs, *earlier)


def attend_backward(base, final, key_len, queries, queries_t, grad, grad_t, attended_t, lse, low_row, bounds, k, v, acc):
    span_len, width = queries.shape
    pairs = pl.cdiv(width, LANES)
    plain = pl.BlockSpec((span_len, LANES), lambda p, b: (0, p))
    turned = pl.BlockSpec((LANES, span_len), lambda p, b: (p, 0))
    low_spec = pl.BlockSpec((1, span_len), lambda p, b: (0, 0))
    key_spec = pl.BlockSpec((k.shape[0], LANES), lambda p, b: (0, p))
    lse_spec = pl.BlockSpec((1, 2, span_len), lambda p, b: (p, 0, 0))
    acc_spec = pl.BlockSpec((1, 2, HEAD, span_len), lambda p, b: (p, 0, 0, 0))
    sums_spec = pl.BlockSpec((2, LANES), lambda p, b: (0, p))
    inputs = (bounds, queries, queries_t, grad, grad_t, attended_t, lse, low_row, k, v)
    specs = [plain, turned, plain, turned, turned, lse_spec, low_spec, key_spec, key_spec]
    if acc is not None:
        inputs += (acc,)
        specs.append(acc_spec)
    sums = jax.ShapeDtypeStruct((span_len, width), BF16) if final else jax.ShapeDtypeStruct((pairs, 2, HEAD, span_len), F32)
    return pl.pallas_call(
        partial(backward_kernel, base, final, pairs, width - (pairs - 1) * LANES, key_len - span_len),
        out_shape=(
            sums,
            jax.ShapeDtypeStruct(k.shape, BF16),
            jax.ShapeDtypeStruct(k.shape, BF16),
            jax.ShapeDtypeStruct((2, width), F32),
        ),
        grid_spec=pltpu.PrefetchScalarGridSpec(
            num_scalar_prefetch=1,
            grid=(pairs,),
            in_specs=specs,
            out_specs=(plain if final else acc_spec, key_spec, key_spec, sums_spec),
            scratch_shapes=[pltpu.VMEM((2, HEAD, span_len), F32)],
        ),
        cost_estimate=pl.CostEstimate(
            flops=40 * span_len * k.shape[0] * width, bytes_accessed=span_len * width, transcendentals=0
        ),
        compiler_params=pltpu.CompilerParams(vmem_limit_bytes=ATTEND_BYTES if k.shape[0] == span_len else VMEM_BYTES),
        name="attend_backward",
    )(*inputs)


def along_group(x, step, count, wrap):
    pairs = [(i, (i + step) % count) for i in range(count) if wrap or 0 <= i + step < count]
    return lax.ppermute(x, "group", pairs)


def hop(rows, step, count):
    bands = rows.reshape(-1, 64, rows.shape[1])
    return along_group(bands, step, count, False).reshape(rows.shape)


def flip(x, bit, count):
    return lax.ppermute(x, "dp", [(i, i ^ bit) for i in range(count)])


CORE, ACROSS, DOWN = 1, 2, 4


def pick(x, index, axis=0):
    return lax.dynamic_index_in_dim(x, index, axis, keepdims=False)


def put(x, part, index):
    start = tuple(index) + (0,) * (x.ndim - len(index))
    part = part.reshape((1,) * len(index) + part.shape)
    return lax.dynamic_update_slice(x, part, start)


def matmul_t(left, right):
    return lax.dot_general(left, right, (((1,), (1,)), ((), ())), preferred_element_type=F32)


def split_rows(core, total_ref, keep_ref, send_ref):
    rows = keep_ref.shape[2]

    def give(first, second):
        for i in range(keep_ref.shape[1]):
            first[0, i] = total_ref[2 * i * rows : (2 * i + 1) * rows, :].astype(BF16)
            second[0, i] = total_ref[(2 * i + 1) * rows : (2 * i + 2) * rows, :].astype(BF16)

    pl.when(core == 0)(lambda: give(keep_ref, send_ref))
    pl.when(core != 0)(lambda: give(send_ref, keep_ref))


def outer_into(left_t, right, total_ref):
    band = total_ref.shape[0] // 4
    for i in range(4):
        total_ref[i * band : (i + 1) * band, :] = jnp.dot(
            left_t[i * band : (i + 1) * band, :], right, preferred_element_type=F32
        )


def feed_kernel(core_ref, x_ref, w_ref, b_ref, g_ref, hidden_ref, slope_ref, keep_ref, send_ref, xt_ref, total_ref):
    @pl.when(pl.program_id(0) == 0)
    def _():
        xt_ref[...] = x_ref[...].T

    span_len = x_ref.shape[0]
    band = span_len // 4
    for i in range(4):
        rows = slice(i * band, (i + 1) * band)
        u = jnp.dot(x_ref[rows, :], w_ref[0], preferred_element_type=F32) + b_ref[0]
        inner = 0.7978845608028654 * (u + 0.044715 * (u * u * u))
        t = jnp.tanh(inner)
        hidden_ref[0, rows, :] = (0.5 * u * (1.0 + t)).astype(BF16)
        slope = 0.5 * (1.0 + t) + 0.5 * u * (1.0 - t * t) * (0.7978845608028654 * (1.0 + 0.134145 * (u * u)))
        slope_ref[0, rows, :] = slope.astype(BF16)
    outer_into(hidden_ref[0].T, g_ref[...], total_ref)
    split_rows(core_ref[0], total_ref, keep_ref, send_ref)


def feed_back_kernel(core_ref, g_ref, wp_ref, slope_ref, xt_ref, wf_ref, keep_ref, send_ref, xg_ref, bg_ref, total_ref):
    grad = matmul_t(g_ref[...], wp_ref[0]) * slope_ref[0].astype(F32)
    low = grad.astype(BF16)
    bg_ref[0] = jnp.sum(low.astype(F32), axis=0, keepdims=True)
    outer_into(xt_ref[...], low, total_ref)
    split_rows(core_ref[0], total_ref, keep_ref, send_ref)
    part = matmul_t(low, wf_ref[0])

    @pl.when(pl.program_id(0) == 0)
    def _():
        xg_ref[...] = part

    @pl.when(pl.program_id(0) != 0)
    def _():
        xg_ref[...] += part


def project_kernel(h_ref, w_ref, r_ref, b_ref, o_ref, total_ref):
    part = jnp.dot(h_ref[0], w_ref[0], preferred_element_type=F32)
    step = pl.program_id(0)

    @pl.when(step == 0)
    def _():
        total_ref[...] = part + (r_ref[...] + b_ref[...])

    @pl.when(step != 0)
    def _():
        total_ref[...] += part

    @pl.when(step == pl.num_programs(0) - 1)
    def _():
        o_ref[...] = total_ref[...].T


def chunk_spec(*shape):
    return pl.BlockSpec((1,) + shape, lambda j, *s: (j,) + (0,) * len(shape))


def whole_spec(*shape):
    return pl.BlockSpec(shape, lambda j, *s: (0,) * len(shape))


def feed_call(kernel, name, scalars, inputs, in_specs, outs, out_specs, scratch, chunks):
    return pl.pallas_call(
        kernel,
        out_shape=outs,
        grid_spec=pltpu.PrefetchScalarGridSpec(
            num_scalar_prefetch=len(scalars),
            grid=(chunks,),
            in_specs=in_specs,
            out_specs=out_specs,
            scratch_shapes=scratch,
        ),
        cost_estimate=pl.CostEstimate(flops=20 * inputs[0].size * inputs[1].shape[-1], bytes_accessed=1024, transcendentals=0),
        compiler_params=pltpu.CompilerParams(vmem_limit_bytes=FULL_BYTES + 4 * 1024 * 1024),
        name=name,
    )(*scalars, *inputs)


def feed(core, x, full_fc, bias, grad):
    span_len, width = x.shape
    chunks = full_fc.shape[0]
    rows = width // 8
    part = jax.ShapeDtypeStruct((chunks, 4, rows, width), BF16)
    tall = jax.ShapeDtypeStruct((chunks, span_len, width), BF16)
    return feed_call(
        feed_kernel,
        "feed",
        (core,),
        (x, full_fc, bias, grad),
        [whole_spec(span_len, width), chunk_spec(width, width), chunk_spec(1, width), whole_spec(span_len, width)],
        (tall, tall, part, part, jax.ShapeDtypeStruct((width, span_len), BF16)),
        (
            chunk_spec(span_len, width),
            chunk_spec(span_len, width),
            chunk_spec(4, rows, width),
            chunk_spec(4, rows, width),
            whole_spec(width, span_len),
        ),
        [pltpu.VMEM((width, width), F32)],
        chunks,
    )


def feed_back(core, grad, full_proj, slope, x_t, full_fc):
    span_len, width = grad.shape
    chunks = full_fc.shape[0]
    rows = width // 8
    part = jax.ShapeDtypeStruct((chunks, 4, rows, width), BF16)
    return feed_call(
        feed_back_kernel,
        "feed_back",
        (core,),
        (grad, full_proj, slope, x_t, full_fc),
        [
            whole_spec(span_len, width),
            chunk_spec(width, width),
            chunk_spec(span_len, width),
            whole_spec(width, span_len),
            chunk_spec(width, width),
        ],
        (part, part, jax.ShapeDtypeStruct((span_len, width), F32), jax.ShapeDtypeStruct((chunks, 1, width), F32)),
        (chunk_spec(4, rows, width), chunk_spec(4, rows, width), whole_spec(span_len, width), chunk_spec(1, width)),
        [pltpu.VMEM((width, width), F32)],
        chunks,
    )


def project(hidden, full_proj, resid, bias):
    chunks, span_len, width = hidden.shape
    return feed_call(
        project_kernel,
        "project",
        (),
        (hidden, full_proj, resid, bias),
        [chunk_spec(span_len, width), chunk_spec(width, width), whole_spec(span_len, width), whole_spec(1, width)],
        jax.ShapeDtypeStruct((width, span_len), F32),
        whole_spec(width, span_len),
        [pltpu.VMEM((span_len, width), F32)],
        chunks,
    )


def after(x, *before):
    return lax.optimization_barrier((x,) + before)[0]


def plane_share_near(mine, count):
    return flip(mine, ACROSS, count), flip(mine, DOWN, count)


def plane_share_far(from_x, from_y, count):
    cut = cut_of(from_x)
    return flip(from_x[:, :, :cut], DOWN, count), flip(from_y[:, :, cut:], ACROSS, count)


def cut_of(part):
    return part.shape[2] // 2 // LANES * LANES


def assemble_kernel(groups, kind, here_ref, own_ref, *refs):
    sources, outs, sems = refs[:10], refs[10:-1], refs[-1]
    chip, core, z = here_ref[0], here_ref[1], here_ref[2]
    cut = sources[3].shape[2]

    def place(index, plane, half):
        if kind == "plane":
            return outs[0].at[plane, index, half]
        if kind == "chip":
            return outs[0].at[index, plane, half]
        return outs[index].at[plane, half]

    def move(index, k, wait):
        n = 1 + k * 2 * (groups - 1)
        for side in range(2):
            half = core if side == 0 else 1 - core
            for step in range(groups - 1):
                target = place(index, lax.rem(z - step - 1 + groups, groups), half)
                if k < 3:
                    pairs = [(sources[side * 5 + k].at[step], target)]
                else:
                    pairs = [
                        (sources[side * 5 + 3].at[step], target.at[:, :cut]),
                        (sources[side * 5 + 4].at[step], target.at[:, cut:]),
                    ]
                for src, dst in pairs:
                    copy = pltpu.make_async_copy(src, dst, sems.at[n])
                    copy.wait() if wait else copy.start()
                    n += 1

    if kind == "plane":
        owns = [(own_ref, outs[0].at[z])]
    elif kind == "chip":
        owns = [(own_ref, outs[0].at[:, z])]
    else:
        owns = [(own_ref.at[m], outs[m].at[z]) for m in range(4)]
    last = sems.shape[0] - len(owns)
    owns = [pltpu.make_async_copy(src, dst, sems.at[last + i]) for i, (src, dst) in enumerate(owns)]
    for copy in owns:
        copy.start()
    for wait in (False, True):
        for k in range(4):
            if kind == "apart":
                for m in range(4):
                    pl.when(chip == m ^ k)(partial(move, m, k, wait))
            else:
                move(chip ^ k, k, wait)
    for copy in owns:
        copy.wait()


def assemble(own, sources, here, groups, kind):
    rows, cols = own.shape[2:]
    if kind == "apart":
        shapes = [(groups, 2, rows, cols)] * 4
    else:
        shapes = [(groups, 4, 2, rows, cols) if kind == "plane" else (4, groups, 2, rows, cols)]
    return pl.pallas_call(
        partial(assemble_kernel, groups, kind),
        out_shape=[jax.ShapeDtypeStruct(shape, own.dtype) for shape in shapes],
        grid_spec=pltpu.PrefetchScalarGridSpec(
            num_scalar_prefetch=1,
            grid=(1,),
            in_specs=[pl.BlockSpec(memory_space=pl.ANY)] * 11,
            out_specs=[pl.BlockSpec(shape, lambda i, h, n=len(shape): (0,) * n) for shape in shapes],
            scratch_shapes=[pltpu.SemaphoreType.DMA((1 + 10 * (groups - 1) + 4,))],
        ),
        compiler_params=pltpu.CompilerParams(vmem_limit_bytes=FULL_BYTES),
        cost_estimate=pl.CostEstimate(flops=0, bytes_accessed=own.size, transcendentals=0),
        name="assemble",
    )(jnp.stack(here).astype(jnp.int32), own, *sources)


def from_planes(piece, groups):
    return jnp.stack([along_group(piece, step, groups, True) for step in range(1, groups)])


def chip_sum(keep, send, count, *during):
    got = flip(send, CORE, count)
    got = after(got, *during) if during else got
    return (keep.astype(F32) + got.astype(F32)).astype(BF16)


def joined(core, keep, send):
    first, second = jnp.where(core == 0, keep, send), jnp.where(core == 0, send, keep)
    both = jnp.stack([first, second], axis=2)
    return both.reshape(both.shape[0], -1, both.shape[-1])


def plane_first_step(half, chip, count, axis):
    to_diag = pick(half, chip ^ 3, axis)
    cut = to_diag.shape[0] // 2
    return flip(to_diag[:cut], ACROSS, count), flip(to_diag[cut:], DOWN, count)


def plane_second_step(half, via, chip, count, axis):
    to_own, to_x, to_y = (pick(half, chip ^ k, axis) for k in range(3))
    cut = to_own.shape[0] // 2
    from_y = flip(jnp.concatenate([to_y[:cut] + via[0], to_y[cut:]]), DOWN, count)
    from_x = flip(jnp.concatenate([to_x[:cut], to_x[cut:] + via[1]]), ACROSS, count)
    return to_own, from_x, from_y


def second_sum(to_own, from_x, from_y):
    return (to_own.astype(F32) + from_x.astype(F32) + from_y.astype(F32)).astype(BF16)


def line_parts(mine, z, groups):
    sent = [(pick(mine, lax.rem(z + step, groups)), step) for step in range(1, groups)]
    return [pick(mine, z)] + [along_group(part, step, groups, True) for part, step in sent]


def parts_sum(parts):
    total = parts[0].astype(F32)
    for part in parts[1:]:
        total = total + part.astype(F32)
    return total


def line_sum(mine, z, groups):
    return parts_sum(line_parts(mine, z, groups))


def shares_of(mine, near, far):
    return jnp.concatenate((mine,) + near + (jnp.concatenate(far, axis=2),))


def in_vmem():
    return pl.BlockSpec(memory_space=pltpu.VMEM)


def norm_back_kernel(parts, turned, values_ref, gain_ref, base_ref, *refs):
    grads, (out_ref, low_ref, gain_sum_ref, shift_sum_ref, low_sum_ref) = refs[:parts], refs[parts:]
    values = values_ref[...].astype(F32)
    grad = grads[0][...].astype(F32)
    for other in grads[1:]:
        grad = grad + other[...].astype(F32)
    center = values - jnp.mean(values, axis=-1, keepdims=True)
    scale = lax.rsqrt(jnp.mean(center * center, axis=-1, keepdims=True) + EPSILON)
    unit = center * scale
    inner = grad * gain_ref[...]
    back = scale * (
        inner - jnp.mean(inner, axis=-1, keepdims=True) - unit * jnp.mean(inner * unit, axis=-1, keepdims=True)
    )
    out = base_ref[...].astype(F32) + back
    out_ref[...] = out.T if turned else out
    low = out.astype(BF16)
    low_ref[...] = low
    sums = (
        jnp.sum(grad * unit, axis=0, keepdims=True),
        jnp.sum(grad, axis=0, keepdims=True),
        jnp.sum(low.astype(F32), axis=0, keepdims=True),
    )
    begun = pl.program_id(0) != 0
    for ref, part in zip((gain_sum_ref, shift_sum_ref, low_sum_ref), sums):
        ref[...] = jnp.where(begun, ref[...], 0.0) + part


def norm_back(values, gain, base, *grads, turned=False):
    span_len, width = values.shape
    band = min(span_len, LANES)
    columns = pl.BlockSpec((width, band), lambda i: (0, i))
    rows = pl.BlockSpec((band, width), lambda i: (i, 0))
    line = pl.BlockSpec((1, width), lambda i: (0, 0))
    sums = jax.ShapeDtypeStruct((1, width), F32)
    out, low, gain_sum, shift_sum, low_sum = pl.pallas_call(
        partial(norm_back_kernel, len(grads), turned),
        out_shape=(
            jax.ShapeDtypeStruct((width, span_len) if turned else (span_len, width), F32),
            jax.ShapeDtypeStruct((span_len, width), BF16),
            sums,
            sums,
            sums,
        ),
        grid=(span_len // band,),
        in_specs=[rows, line, rows] + [rows] * len(grads),
        out_specs=(columns if turned else rows, rows, line, line, line),
        cost_estimate=pl.CostEstimate(flops=0, bytes_accessed=1024, transcendentals=0),
        compiler_params=pltpu.CompilerParams(vmem_limit_bytes=VMEM_BYTES),
        name="norm_back",
    )(values, gain[None], base, *grads)
    return out, low, gain_sum, shift_sum, low_sum


def key_back_kernel(dk_ref, dv_ref, wk_ref, wv_ref, *refs):
    out_ref = refs[-1]
    total = matmul_t(dk_ref[...], wk_ref[...]) + matmul_t(dv_ref[...], wv_ref[...])
    for other in refs[:-1]:
        total = total + other[...].astype(F32)
    out_ref[...] = total.astype(out_ref.dtype)


def key_back(dk, dv, full_k, full_v, moving, kind):
    more = () if moving is None else (moving,)
    return pl.pallas_call(
        key_back_kernel,
        out_shape=jax.ShapeDtypeStruct(dk.shape, kind),
        in_specs=[in_vmem()] * (4 + len(more)),
        out_specs=in_vmem(),
        cost_estimate=pl.CostEstimate(flops=0, bytes_accessed=1024, transcendentals=0),
        compiler_params=pltpu.CompilerParams(vmem_limit_bytes=VMEM_BYTES),
        name="key_back",
    )(dk, dv, full_k, full_v, *more)


def attn_grads_kernel(blocks, core_ref, *refs):
    normed, dks, dvs = refs[:blocks], refs[blocks : 2 * blocks], refs[2 * blocks : 3 * blocks]
    dq_ref, ot_ref, low_ref, keep_ref, send_ref, total_ref, turned_ref = refs[3 * blocks :]
    span_len = dq_ref.shape[0]
    step = pl.program_id(0)
    width = total_ref.shape[0]
    band = width // 4

    def sums(rights):
        for i in range(4):
            rows = slice(i * band, (i + 1) * band)
            total = None
            for b, right in enumerate(rights):
                if right is None:
                    continue
                part = jnp.dot(turned_ref[b, rows, :], right, preferred_element_type=F32)
                total = part if total is None else total + part
            total_ref[rows, :] = total

    @pl.when(step == 0)
    def _():
        begin = 0
        for ref in normed:
            for at in range(0, ref.shape[0], span_len):
                turned_ref[begin // span_len] = ref[at : at + span_len, :].T
                begin += span_len
        sums([None] * (turned_ref.shape[0] - 1) + [dq_ref[...]])

    def pieces(group):
        return [ref[at : at + span_len, :] for ref in group for at in range(0, ref.shape[0], span_len)]

    pl.when(step == 1)(lambda: sums(pieces(dks)))
    pl.when(step == 2)(lambda: sums(pieces(dvs)))

    @pl.when(step == 3)
    def _():
        outer_into(ot_ref[...], low_ref[...], total_ref)

    split_rows(core_ref[0], total_ref, keep_ref, send_ref)


def attn_grads(core, normed, dks, dvs, dq, attended_t, low):
    span_len, width = dq.shape
    rows = width // 8
    key_len = sum(block.shape[0] for block in normed)
    part = jax.ShapeDtypeStruct((4, 4, rows, width), BF16)
    inputs = (*normed, *dks, *dvs, dq, attended_t, low)
    return pl.pallas_call(
        partial(attn_grads_kernel, len(normed)),
        out_shape=(part, part),
        grid_spec=pltpu.PrefetchScalarGridSpec(
            num_scalar_prefetch=1,
            grid=(4,),
            in_specs=[in_vmem()] * len(inputs),
            out_specs=(chunk_spec(4, rows, width), chunk_spec(4, rows, width)),
            scratch_shapes=[
                pltpu.VMEM((width, width), F32),
                pltpu.VMEM((key_len // span_len, width, span_len), BF16),
            ],
        ),
        cost_estimate=pl.CostEstimate(flops=20 * span_len * width * width, bytes_accessed=1024, transcendentals=0),
        compiler_params=pltpu.CompilerParams(vmem_limit_bytes=56 * 1024 * 1024),
        name="attn_grads",
    )(core, *inputs)


def give_out_kernel(kind, here_ref, mine_ref, other_ref, *outs):
    chip, core = here_ref[0], here_ref[1]
    rows, cols = mine_ref.shape[1:]
    for side, ref in enumerate((mine_ref, other_ref)):
        half = core if side == 0 else 1 - core
        for k in range(4):
            piece = ref[k].astype(F32)
            if kind == "plane":
                at = pl.ds(pl.multiple_of(((chip ^ k) * 2 + half) * rows, 8), rows)
                outs[0][at, :] = piece
                continue
            at = pl.ds(pl.multiple_of(half * rows, 8), rows)
            for m in range(4):

                @pl.when(chip == m ^ k)
                def _(m=m, at=at, piece=piece):
                    if kind == "apart":
                        outs[m][at, :] = piece
                    else:
                        outs[0][at, m * cols : (m + 1) * cols] = piece


def give_out(shares, other, here, kind):
    rows, cols = shares.shape[1:]
    shapes = {"apart": [(2 * rows, cols)] * 4, "chip": [(2 * rows, 4 * cols)], "plane": [(8 * rows, cols)]}[kind]
    return pl.pallas_call(
        partial(give_out_kernel, kind),
        out_shape=[jax.ShapeDtypeStruct(shape, F32) for shape in shapes],
        grid_spec=pltpu.PrefetchScalarGridSpec(
            num_scalar_prefetch=1,
            grid=(1,),
            in_specs=[whole_spec(4, rows, cols)] * 2,
            out_specs=[whole_spec(*shape) for shape in shapes],
        ),
        cost_estimate=pl.CostEstimate(flops=0, bytes_accessed=1024, transcendentals=0),
        compiler_params=pltpu.CompilerParams(vmem_limit_bytes=VMEM_BYTES),
        name="give_out",
    )(jnp.stack(here).astype(jnp.int32), shares, other)


def enter_kernel(own, x_ref, gain_ref, shift_ref, wk_ref, wv_ref, bv_ref, *refs):
    values = x_ref[...].astype(F32)
    center = values - jnp.mean(values, axis=-1, keepdims=True)
    scale = lax.rsqrt(jnp.mean(center * center, axis=-1, keepdims=True) + EPSILON)
    normed = (center * scale * gain_ref[...] + shift_ref[...]).astype(BF16)
    if own:
        wq_ref, bq_ref, n_ref, k_ref, v_ref, q_ref, qt_ref = refs
        q = (jnp.dot(normed, wq_ref[...], preferred_element_type=F32) + bq_ref[...]).astype(BF16)
        q_ref[...] = q
        qt_ref[...] = q.T
    else:
        n_ref, k_ref, v_ref = refs
    n_ref[...] = normed
    k_ref[...] = jnp.dot(normed, wk_ref[...], preferred_element_type=F32).astype(BF16)
    v_ref[...] = (jnp.dot(normed, wv_ref[...], preferred_element_type=F32) + bv_ref[...]).astype(BF16)


def enter(x, gain, shift, full_k, full_v, bias_v, *query):
    span_len, width = x.shape
    band = span_len
    rows = pl.BlockSpec((band, width), lambda i: (i, 0))
    line = pl.BlockSpec((1, width), lambda i: (0, 0))
    inputs = [x, gain[None], shift[None], full_k, full_v, bias_v[None]]
    in_specs = [rows, line, line, in_vmem(), in_vmem(), line]
    shapes, out_specs = [(span_len, width)] * 3, [rows] * 3
    if query:
        inputs += [query[0], query[1][None]]
        in_specs += [in_vmem(), line]
        shapes += [(span_len, width), (width, span_len)]
        out_specs += [rows, pl.BlockSpec((width, band), lambda i: (0, i))]
    return pl.pallas_call(
        partial(enter_kernel, bool(query)),
        out_shape=[jax.ShapeDtypeStruct(shape, BF16) for shape in shapes],
        grid=(span_len // band,),
        in_specs=in_specs,
        out_specs=out_specs,
        cost_estimate=pl.CostEstimate(flops=0, bytes_accessed=1024, transcendentals=0),
        compiler_params=pltpu.CompilerParams(vmem_limit_bytes=FULL_BYTES),
        name="enter",
    )(*inputs)


def mean_spread(values):
    center = values - jnp.mean(values, axis=-1, keepdims=True)
    spread = jnp.mean(center * center, axis=-1, keepdims=True)
    return center, lax.rsqrt(spread + EPSILON)


def layer_norm(values, gain, shift):
    center, scale = mean_spread(values)
    return center * scale * gain + shift


def layer_norm_back(values, gain, grad):
    center, scale = mean_spread(values)
    unit = center * scale
    inner = grad * gain
    back = scale * (
        inner
        - jnp.mean(inner, axis=-1, keepdims=True)
        - unit * jnp.mean(inner * unit, axis=-1, keepdims=True)
    )
    return back, jnp.sum(grad * unit, axis=0), jnp.sum(grad, axis=0)


def row_sum(values):
    return jnp.sum(values.astype(F32), axis=0)


def matmul(left, right):
    return jnp.dot(left, right, preferred_element_type=F32)


def weight_grad(left, right):
    return jnp.einsum("ra,rb->ab", left, right, preferred_element_type=F32).astype(BF16)


def back_through(grad_rows, weight):
    return jnp.einsum("rb,ab->ra", grad_rows, weight, preferred_element_type=F32)


def on_device(
    count,
    groups,
    tokens,
    segments,
    out_grad,
    norm1_gain,
    norm1_bias,
    w_query,
    query_bias,
    w_key,
    w_value,
    value_bias,
    w_out,
    out_bias,
    norm2_gain,
    norm2_bias,
    w_fc,
    fc_bias,
    w_proj,
    proj_bias,
):
    _, span_len, width = tokens.shape
    shard = width // groups
    half = shard // 2
    chunks = w_fc.shape[1] // width
    key_len = segments.shape[1]
    z = lax.axis_index("group")
    place = lax.axis_index("dp")
    fast = count == 8 and groups == 4 and chunks == 4
    chip, core = place // 2, lax.rem(place, 2)
    here = (chip, core, z)
    forward_parts = attend_parts(pl.cdiv(width, LANES), 3)

    small = jnp.concatenate(
        [norm1_gain, norm1_bias, query_bias, value_bias, out_bias, norm2_gain, norm2_bias, proj_bias, fc_bias]
    )
    if fast:
        attn_mats = [w.reshape(2, half, width) for w in (w_query, w_key, w_value, w_out)]
        attn_piece = lax.select_n(chip, *(pick(w, core) for w in attn_mats))
        attn_hops = [along_group(attn_piece, step, groups, True) for step in range(1, groups)]
        small = after(small, attn_hops[0])
    small_rel = jnp.stack([small] + [along_group(small, step, groups, True) for step in range(1, groups)])
    small_all = jnp.take(small_rel, lax.rem(z - jnp.arange(groups) + groups, groups), axis=0)
    vectors = small_all[:, : 8 * shard].reshape(groups, 8, shard).transpose(1, 0, 2).reshape(8, width)
    gain_one, shift_one, bias_q, bias_v, bias_o, gain_two, shift_two, bias_p = vectors.astype(F32)
    bias_fc = small_all[:, 8 * shard :].astype(F32).reshape(chunks, 1, width)

    mine = tokens[0]
    inputs = mine.astype(F32)
    own_base = key_len - span_len
    if fast:
        attn_own = jnp.stack(attn_mats)
        attn_ring = jnp.stack(attn_hops)
        attn_near = plane_share_near(attn_ring, count)
        hops = [mine, hop(after(mine, attn_ring, small_rel), 1, groups)]
        attn_three = (attn_ring,) + attn_near
        attn_far = plane_share_far(*attn_near, count)
        attn_other = tuple(flip(after(part, *attn_near), CORE, count) for part in attn_three)
        attn_other += tuple(flip(after(part, hops[1]), CORE, count) for part in attn_far)
        hops.append(hop(hops[1], 1, groups))
        attn = assemble(attn_own, attn_three + attn_far + attn_other, here, groups, "apart")
        full_q, full_k, full_v, full_o = (part.reshape(width, width) for part in attn)
        hops.append(hop(hops[2], 1, groups))
    else:
        gather = partial(lax.all_gather, axis_name="group", axis=0, tiled=True)
        full_q, full_k, full_v, full_o = (gather(w) for w in (w_query, w_key, w_value, w_out))
        full_fc = gather(w_fc).reshape(width, chunks, width).transpose(1, 0, 2)
        full_proj = gather(w_proj).reshape(chunks, width, width)
    if fast:
        known = (gain_one, shift_one, full_k, full_v, bias_v)
        *own, queries, queries_t = enter(after(mine, hops[2]), *known, full_q, bias_q)
        second = enter(after(hops[1], queries), *known)
        third = enter(after(hops[2], second[1]), *known)
        fc_own = w_fc.reshape(2, half, chunks, width).transpose(2, 0, 1, 3)
        fc_piece = pick(pick(fc_own, chip), core)
        proj_own = w_proj.reshape(4, 2, half, width)
        proj_piece = pick(pick(proj_own, chip), core)
        hops[3] = after(hops[3], third[1])
        fc_ring = from_planes(after(fc_piece, hops[3]), groups)
        blocks = [enter(hops[3], *known), third, second, own]
        normed, keys, values = ([block[i] for block in blocks] for i in range(3))
    else:
        hops = [mine]
        for _ in range(groups - 1):
            hops.append(hop(hops[-1], 1, groups))
        normed = [layer_norm(jnp.concatenate(hops[::-1]).astype(F32), gain_one, shift_one).astype(BF16)]
        keys = [matmul(normed[0], full_k).astype(BF16)]
        values = [(matmul(normed[0], full_v) + bias_v).astype(BF16)]
        queries = (matmul(normed[0][own_base:], full_q) + bias_q).astype(BF16)
        queries_t = queries.T

    seg = segments[0]
    seg_mine = lax.dynamic_slice_in_dim(seg, z * span_len, span_len)
    low_row = jnp.sum((seg[None, :] < seg_mine[:, None]).astype(jnp.int32), axis=1)
    low_row = low_row + (groups - 1 - z) * span_len
    bounds = jnp.stack([low_row[0], low_row[-1]]).astype(jnp.int32)
    low_row = low_row[None]

    state = None
    for number, part in enumerate(forward_parts):
        row_now = low_row
        if fast and number == 1:
            fc_near = plane_share_near(after(fc_ring, state[0]), count)
            proj_ring = from_planes(after(proj_piece, fc_ring, state[0]), groups)
            row_now = after(low_row, fc_ring)
        if fast and number == 2:
            fc_three = (fc_ring,) + fc_near
            fc_far = plane_share_far(*(after(part, state[0]) for part in fc_near), count)
            fc_other = tuple(flip(after(part, state[0], *fc_near), CORE, count) for part in fc_three)
            row_now = after(low_row, proj_ring, *fc_near)
        state = attend_forward(part, queries_t, keys, values, row_now, bounds, state)
    attended_t, lse = state
    if fast:
        attended_t, *fc_moved = lax.optimization_barrier((attended_t, *fc_far, *fc_other))
        fc_far, fc_other = tuple(fc_moved[:2]), tuple(fc_moved[2:])
        fc_other += tuple(flip(part, CORE, count) for part in fc_far)
        proj_near = plane_share_near(after(proj_ring, attended_t), count)
    resid = inputs + jnp.einsum("ft,fd->td", attended_t, full_o, preferred_element_type=F32) + bias_o
    normed_two = layer_norm(resid, gain_two, shift_two).astype(BF16)
    if fast:
        full_fc = assemble(after(fc_own, normed_two), fc_three + fc_far + fc_other, here, groups, "chip")
        full_fc = full_fc[0].reshape(4, width, width)

    cot = out_grad[0]
    proj_bias_grad = row_sum(cot)
    which = jnp.reshape(core, (1,)).astype(jnp.int32)
    if fast:
        proj_three = (proj_ring,) + proj_near
        proj_far = plane_share_far(*(after(part, full_fc) for part in proj_near), count)
        proj_other = tuple(flip(after(part, full_fc, *proj_near), CORE, count) for part in proj_three)
        normed_two = after(normed_two, *proj_near)
    hidden, slope, proj_keep, proj_send, normed_two_t = feed(which, normed_two, full_fc, bias_fc, cot)
    cot_now = cot
    if fast:
        proj_send, *proj_moved = lax.optimization_barrier((proj_send, *proj_far, *proj_other))
        proj_far, proj_other = tuple(proj_moved[:2]), tuple(proj_moved[2:])
        proj_other += tuple(flip(part, CORE, count) for part in proj_far)
        proj_send = after(proj_send, *proj_other)
        full_proj = assemble(proj_own, proj_three + proj_far + tuple(proj_other), here, groups, "plane")
        full_proj = full_proj[0].reshape(4, width, width)
        proj_chip = chip_sum(proj_keep, proj_send, count)
        cot_now, proj_chip = lax.optimization_barrier((cot, proj_chip))
        proj_via = plane_first_step(proj_chip, chip, count, 1)
    fc_keep, fc_send, normed_two_grad, fc_bias_grad = feed_back(which, cot_now, full_proj, slope, normed_two_t, full_fc)
    if fast:
        normed_two_grad = after(normed_two_grad, *proj_via)
    resid_grad, resid_low, gain_two_grad, shift_two_grad, out_bias_grad = norm_back(
        resid, gain_two, cot, normed_two_grad
    )
    attended_grad = back_through(resid_low, full_o).astype(BF16)
    attended_grad_t = jnp.einsum("td,fd->ft", resid_low, full_o, preferred_element_type=F32).astype(BF16)
    if fast:
        proj_mine = plane_second_step(proj_chip, proj_via, chip, count, 1)
        fc_chip = chip_sum(fc_keep, after(fc_send, *proj_via), count, attended_grad)
        fc_via = plane_first_step(fc_chip, chip, count, 0)
    acc, moving, base = None, None, 0
    dks, dvs, value_bias_grad = [], [], 0.0
    for number, (k, v) in enumerate(zip(keys, values)):
        row_now = low_row
        final = number == len(keys) - 1
        if fast and number == 0:
            row_now = after(low_row, fc_chip)
        if fast and number == 1:
            row_now = after(low_row, sent, proj_mine)
        if fast and number == 2:
            row_now = after(low_row, sent, proj_line)
        if fast and number == 3:
            row_now = after(low_row, sent, fc_mine, *proj_line_near)
        acc, dk, dv, sums = attend_backward(
            base, final, key_len, queries, queries_t, attended_grad, attended_grad_t, attended_t, lse, row_now, bounds, k, v, acc
        )
        base += k.shape[0]
        dks.append(dk)
        dvs.append(dv)
        value_bias_grad = value_bias_grad + sums[:1]
        if final:
            break
        if number > 0:
            moving = after(moving, acc)
        sent = key_back(dk, dv, full_k, full_v, moving, BF16)
        if number == 0:
            sent = after(sent, *fc_via)
        moving = hop(sent, -1, groups)
        if number == 0:
            proj_mine = second_sum(*(after(part, sent) for part in proj_mine))
            proj_lines = line_parts(proj_mine, z, groups)
        if number == 1:
            proj_line = parts_sum([after(part, sent) for part in proj_lines]).astype(BF16)
            proj_line_near = plane_share_near(proj_line[None], count)
            fc_mine = plane_second_step(fc_chip, fc_via, chip, count, 0)
        if number == 2:
            fc_mine = second_sum(*(after(part, sent) for part in fc_mine))
            proj_line_near = tuple(after(part, sent) for part in proj_line_near)
            proj_line_far = plane_share_far(*proj_line_near, count)
    dqueries, query_bias_grad = acc, sums[1:]
    dqueries_now = dqueries
    if fast:
        norm_term = key_back(dk, dv, full_k, full_v, after(moving, acc), F32)
        fc_lines = line_parts(after(fc_mine, norm_term), z, groups)
        proj_line_far = tuple(after(part, norm_term) for part in proj_line_far)
        proj_shares = shares_of(proj_line[None], proj_line_near, proj_line_far)
        proj_others = flip(proj_shares, CORE, count)
        dqueries_now = after(dqueries, norm_term, *proj_line_far)
    else:
        norm_term = back_through(dk, full_k) + back_through(dv, full_v)
        for step in range(groups - 1):
            part = norm_term[step * span_len : (step + 1) * span_len]
            moving = hop((part if moving is None else part + moving.astype(F32)).astype(BF16), -1, groups)
        norm_term = norm_term[own_base:] + moving.astype(F32)
    attn_keep, attn_send = attn_grads(which, normed, dks, dvs, dqueries_now, attended_t, resid_low)
    dqueries_now = dqueries
    if fast:
        fc_line = parts_sum([after(part, attn_send) for part in fc_lines]).astype(BF16)
        attn_chip = chip_sum(attn_keep, after(attn_send, fc_line), count)
        fc_line_near = plane_share_near(fc_line[None], count)
        attn_via = plane_first_step(attn_chip, chip, count, 0)
        fc_line_near = tuple(after(part, attn_chip) for part in fc_line_near)
        fc_line_far = plane_share_far(*fc_line_near, count)
        (proj_sum,) = give_out(after(proj_shares, attn_chip), proj_others, here, "plane")
        attn_mine = plane_second_step(after(attn_chip, proj_sum), attn_via, chip, count, 0)
        fc_line_far = tuple(after(part, *attn_via) for part in fc_line_far)
        fc_shares = shares_of(fc_line[None], fc_line_near, fc_line_far)
        fc_others = flip(fc_shares, CORE, count)
        dqueries_now = after(dqueries, *attn_via)
    normed_one_grad = back_through(dqueries_now, full_q)
    tokens_grad, _, gain_one_grad, shift_one_grad, _ = norm_back(
        mine, gain_one, resid_grad, normed_one_grad, norm_term, turned=True
    )
    vector_sums = jnp.concatenate(
        [
            gain_one_grad,
            shift_one_grad,
            query_bias_grad,
            value_bias_grad,
            out_bias_grad,
            gain_two_grad,
            shift_two_grad,
            proj_bias_grad[None],
            fc_bias_grad.reshape(chunks, width),
        ]
    )
    vector_sums = parts_sum([vector_sums] + [along_group(vector_sums, step, groups, True) for step in range(1, groups)])
    hidden_now = hidden
    if fast:
        attn_mine = second_sum(*(after(part, tokens_grad) for part in attn_mine))
        attn_line = line_parts(attn_mine, z, groups)
        vector_sums = vector_sums + flip(vector_sums, CORE, count)
        hidden_now = after(hidden, attn_mine, vector_sums)
    activations = project(hidden_now, full_proj, resid, bias_p[None])
    if fast:
        vector_sums = vector_sums + after(flip(vector_sums, ACROSS, count), activations)
        (fc_sum,) = give_out(after(fc_shares, activations), fc_others, here, "chip")
        attn_line = [after(part, vector_sums, fc_sum) for part in attn_line]
        vector_sums = vector_sums + flip(vector_sums, DOWN, count)
    else:
        bit = 1
        while bit < count:
            vector_sums = vector_sums + flip(vector_sums, bit, count)
            bit *= 2
    if fast:
        attn_line = parts_sum([after(part, activations) for part in attn_line]).astype(BF16)
        attn_near = plane_share_near(attn_line[None], count)
        attn_far = plane_share_far(*attn_near, count)
        attn_shares = shares_of(attn_line[None], attn_near, attn_far)
        attn_others = flip(attn_shares, CORE, count)
        q_sum, k_sum, v_sum, out_sum = give_out(attn_shares, attn_others, here, "apart")

    eight = lax.dynamic_slice_in_dim(vector_sums[:8], z * shard, shard, 1)
    fc_bias_sum = lax.dynamic_slice_in_dim(vector_sums[8:].reshape(-1), z * fc_bias.shape[0], fc_bias.shape[0])
    if not fast:

        def whole_sum(part):
            part = lax.psum_scatter(part, "group", scatter_dimension=0, tiled=True)
            return lax.psum(part.astype(F32), "dp")

        proj_sum = whole_sum(joined(core, proj_keep, proj_send).reshape(chunks * width, width))
        fc_sum = whole_sum(joined(core, fc_keep, fc_send).transpose(1, 0, 2).reshape(width, chunks * width))
        attn_whole = joined(core, attn_keep, attn_send)
        q_sum, k_sum, v_sum, out_sum = (whole_sum(attn_whole[m]) for m in range(4))
    return (
        activations.T[None],
        tokens_grad.T[None],
        eight[0],
        eight[1],
        q_sum,
        eight[2],
        k_sum,
        v_sum,
        eight[3],
        out_sum,
        eight[4],
        eight[5],
        eight[6],
        fc_sum,
        fc_bias_sum,
        proj_sum,
        eight[7],
    )


def solution(mesh):
    rows, vec, mat = P("dp", "group", None), P("group"), P("group", None)
    weights = (vec, vec, mat, vec, mat, mat, vec, mat, vec, vec, vec, mat, vec, mat, vec)
    return jax.shard_map(
        partial(on_device, mesh.shape["dp"], mesh.shape["group"]),
        mesh=mesh,
        in_specs=(rows, P("dp", None), rows) + weights,
        out_specs=(rows, rows) + weights,
        check_vma=False,
    )
```
